128 devices in a mesh: group: 8 (over y, z_lo), dev: 16 (over z_hi, x, core).
Axes of the slice: x: 4, y: 4, z: 4 (z_hi: 2, z_lo: 2; z = z_hi * 2 + z_lo), core: 2. Of those that a mesh axis runs over, the one named last changes fastest.
Arguments:
- member_pressure_heads: float32 [192, 512, 768], P('group', 'dev'), may hold values from -4 to 1
- soil_index: int32 [512, 768], P('dev'), may hold values from 0 to 7
- ks_table: float32 [8], replicated, may hold values from 0.05 to 0.5
- alpha_table: float32 [8], replicated, may hold values from 0.5 to 3
- obs_op: float32 [512, 6, 32, 128], P(('dev', 'group')), may hold values from -0.09375 to 0.09375
- obs_mask: int32 [512, 6], P(('dev', 'group')), may hold values from 0 to 1
- obs_values: float32 [512, 6, 32], P(('dev', 'group')), may hold values from -6 to 6
Outputs:
- analysis: float32 [192, 512, 768], P('group', 'dev')
The draws below stay inside these ranges and needn't reach their ends.
All inputs are finite; a program needn't handle non-finite values.
Results may differ from the reference program's by a relative error of at most 0.0003.
Values sent between devices are 32-bit elements; how exact they have to be, the bound alone decides.
No kernel may reach another device: no remote copies, remote signals or barrier semaphores. Data moves between devices by JAX's collectives and lax.ppermute only.
A program may use at most 64 MiB of HBM per device.

```python
import math
import jax
import jax.numpy as jnp
from jax import lax

MEMBERS = 192
COLUMNS = 768
OBS_BLOCK = 32
SOIL_TYPES = 8
MODEL_STEPS = 3
NEWTON_STEPS = 12
BLOCKS = 6
GRID_ROWS = 512


def draw_member_pressure_heads(key, part):
    key_base = jax.random.fold_in(key, 11)
    key_scale = jax.random.fold_in(key, 12)
    key_noise = jax.random.fold_in(key, 13)
    key_modes = jax.random.fold_in(key, 14)
    key_loads = jax.random.fold_in(key, 15)
    mode_count = 4
    base_field = jax.random.uniform(key_base, (1, GRID_ROWS, COLUMNS), jnp.float32, -2.5, -0.5)
    member_scale = jnp.exp(jax.random.uniform(key_scale, (MEMBERS, 1, 1), jnp.float32, jnp.log(0.02), jnp.log(0.5)))
    mode_fields = jax.random.normal(key_modes, (mode_count, GRID_ROWS * COLUMNS), jnp.float32)
    loadings = jax.random.normal(key_loads, (MEMBERS, mode_count), jnp.float32)
    shared_part = jnp.dot(loadings, mode_fields, precision=jax.lax.Precision.HIGHEST) / jnp.sqrt(mode_count * 1.0)
    shared_part = shared_part.reshape(MEMBERS, GRID_ROWS, COLUMNS)
    own_part = jax.random.normal(key_noise, (MEMBERS, GRID_ROWS, COLUMNS), jnp.float32)
    share_weight = 0.5
    noise_field = jnp.sqrt(1.0 - share_weight) * own_part + jnp.sqrt(share_weight) * shared_part
    noise_field = jnp.clip(noise_field, -3.0, 3.0)
    return base_field + member_scale * noise_field


def draw_obs_mask(key, part):
    random_draws = jax.random.randint(jax.random.fold_in(key, 23), (GRID_ROWS, BLOCKS), 0, 4 * GRID_ROWS, dtype=jnp.int32)
    thresholds = GRID_ROWS + 2 * jnp.arange(GRID_ROWS, dtype=jnp.int32)
    return (random_draws < thresholds[:, None]).astype(jnp.int32)


def with_ends(values, own_key, least, largest):
    shape = values.shape
    place = [jax.random.randint(jax.random.fold_in(own_key, axis), (), 0, shape[axis]) for axis in range(len(shape))]
    values = values.at[tuple(place)].set(least)
    longest = shape.index(max(shape))
    place[longest] = (place[longest] + 1) % shape[longest]
    return values.at[tuple(place)].set(largest)


def levels(stream_key, extent, shards, smallest, high):
    loudness = 1.0
    for axis_at, blocks in shards:
        steps = jax.random.uniform(jax.random.fold_in(jax.random.fold_in(stream_key, 6), axis_at), (blocks,), jnp.float32, smallest / len(shards), high / len(shards))
        loudness = loudness * jnp.repeat(jnp.exp(steps), extent[axis_at] // blocks).reshape((-1,) + (1,) * (len(extent) - 1 - axis_at))
    return loudness


def noise(key, extent, spread, reach, shards=(), kind=jnp.bfloat16):
    values = spread * jax.random.normal(key, extent, jnp.float32)
    if shards:
        values = values * levels(key, extent, shards, -0.22, 0.18)
    return jnp.clip(values, -reach, reach).astype(kind)


def setup_inputs(seed: int = 0) -> dict:
    splits = jax.random.split(jax.random.key(seed), 8)
    member_pressure_heads = draw_member_pressure_heads(jax.random.fold_in(splits[7], 71), 0)
    soil_index = with_ends(jax.random.randint(splits[1], (GRID_ROWS, COLUMNS), 0, SOIL_TYPES), jax.random.fold_in(splits[1], 1), 0, SOIL_TYPES - 1).astype(jnp.int32)
    ks_table = jnp.clip(jnp.exp(jax.random.uniform(splits[2], (SOIL_TYPES,), jnp.float32, math.log(0.05), math.log(0.5))), 0.05, 0.5)
    alpha_table = jnp.clip(jnp.exp(jax.random.uniform(splits[3], (SOIL_TYPES,), jnp.float32, math.log(0.5), math.log(3.0))), 0.5, 3.0)
    obs_op = noise(splits[4], (GRID_ROWS, BLOCKS, OBS_BLOCK, 128), (128 * max(1, GRID_ROWS * BLOCKS * OBS_BLOCK // (16 * MEMBERS))) ** -0.5, 0.09375, ((0, 128),), jnp.float32)
    obs_mask = draw_obs_mask(jax.random.fold_in(splits[7], 71), 0)
    obs_values = noise(splits[6], (GRID_ROWS, BLOCKS, OBS_BLOCK), 1.0, 6.0, ((0, 128),), jnp.float32)
    return dict(member_pressure_heads=member_pressure_heads, soil_index=soil_index, ks_table=ks_table, alpha_table=alpha_table, obs_op=obs_op, obs_mask=obs_mask, obs_values=obs_values)


step_duration = 0.1
gravity_head = 1.0
highest = lax.Precision.HIGHEST

def soil_values(soil_index, ks_table, alpha_table):
    soil_kinds = jnp.arange(SOIL_TYPES, dtype=jnp.int32)
    one_hot = (soil_index[None] == soil_kinds[:, None, None]).astype(jnp.float32)
    hydraulic_conductance = lax.optimization_barrier(jnp.sum(one_hot * ks_table[:, None, None], axis=0))
    retention_shape = lax.optimization_barrier(jnp.sum(one_hot * alpha_table[:, None, None], axis=0))
    return (hydraulic_conductance, retention_shape)

def soil_hydraulic_law(heads_now, hydraulic_conductance, retention_shape):
    factor = jnp.exp(retention_shape * jnp.minimum(heads_now, 0.0))
    return (hydraulic_conductance * factor, 0.1 + 0.4 * retention_shape * factor)

def surface_recharge(padded_heads, padded_k):
    middle = padded_heads[:, 1:-1]
    k_middle = padded_k[:, 1:-1]
    across = 0.5 * (k_middle + padded_k[:, 2:]) * (padded_heads[:, 2:] - middle)
    across = across + 0.5 * (k_middle + padded_k[:, :-2]) * (padded_heads[:, :-2] - middle)
    k_face = 0.5 * (k_middle[..., 1:] + k_middle[..., :-1])
    vertical = k_face * (middle[..., 1:] - middle[..., :-1] - gravity_head)
    border = jnp.zeros_like(middle[..., :1])
    return across + jnp.concatenate([vertical, border], -1) - jnp.concatenate([border, vertical], -1)

def newton_weights(gram_matrix, gram_rhs):
    order_m = gram_matrix.shape[0]
    identity_m = jnp.eye(order_m, dtype=jnp.float32)
    norm_total = jnp.sum(jnp.abs(gram_matrix))

    def one_turn(counter, iterate_pair):
        iterate, inverse = iterate_pair
        middle = 0.5 * (3.0 * identity_m - jnp.dot(inverse, iterate, precision=highest, preferred_element_type=jnp.float32))
        return (jnp.dot(iterate, middle, precision=highest, preferred_element_type=jnp.float32), jnp.dot(middle, inverse, precision=highest, preferred_element_type=jnp.float32))
    iterate, inverse = lax.fori_loop(0, NEWTON_STEPS, one_turn, (gram_matrix / norm_total, identity_m))
    inner_w = jnp.dot(inverse, gram_rhs, precision=highest, preferred_element_type=jnp.float32)
    shift_w = jnp.dot(inverse, inner_w, precision=highest, preferred_element_type=jnp.float32) / norm_total
    return jnp.sqrt((order_m - 1.0) / norm_total) * inverse + shift_w[:, None]

def reference(member_pressure_heads, soil_index, ks_table, alpha_table, obs_op, obs_mask, obs_values):
    hydraulic_conductance, retention_shape = soil_values(soil_index, ks_table, alpha_table)
    predict_heads = member_pressure_heads
    layer_widths = ((0, 0), (1, 1), (0, 0))
    for counter in range(MODEL_STEPS):
        conductivity_field, moisture_capacity = soil_hydraulic_law(predict_heads, hydraulic_conductance, retention_shape)
        predict_heads = predict_heads + step_duration * surface_recharge(jnp.pad(predict_heads, layer_widths), jnp.pad(conductivity_field, layer_widths)) / moisture_capacity
    ensemble_average = lax.optimization_barrier(jnp.mean(predict_heads, axis=0))
    member_anomalies = predict_heads - ensemble_average
    mask_float = obs_mask.astype(jnp.float32)
    masked_op = obs_op * mask_float[:, :, None, None]
    projected = jnp.einsum('rboc,mrbc->rbom', masked_op, member_anomalies.reshape(MEMBERS, GRID_ROWS, BLOCKS, 128), precision=highest).reshape(-1, MEMBERS)
    innovation = (obs_values * mask_float[:, :, None] - jnp.einsum('rboc,rbc->rbo', masked_op, ensemble_average.reshape(GRID_ROWS, BLOCKS, 128), precision=highest)).reshape(-1)
    identity_m = jnp.eye(MEMBERS, dtype=jnp.float32)
    gram_matrix = jnp.dot(projected.T, projected, precision=highest, preferred_element_type=jnp.float32) + (MEMBERS - 1.0) * identity_m
    gram_rhs = jnp.dot(projected.T, innovation, precision=highest, preferred_element_type=jnp.float32)
    mixing = newton_weights(gram_matrix, gram_rhs)
    mixed = jnp.dot(mixing.T, member_anomalies.reshape(MEMBERS, -1), precision=highest, preferred_element_type=jnp.float32)
    return mixed.reshape(MEMBERS, GRID_ROWS, COLUMNS)
```

```python
import jax
import jax.numpy as jnp
from jax import lax
from jax.experimental import pallas as pl
from jax.experimental.pallas import tpu as pltpu
from jax.sharding import PartitionSpec as P

MEMBERS = 192
SOIL_TYPES = 8
MODEL_STEPS = 3
NEWTON_STEPS = 12
BLOCKS = 6
OBS = 32

step_duration = 0.1
gravity_head = 1.0
AXES = ("group", "dev")


def soil_values(soil_index, ks_table, alpha_table):
    soil_kinds = jnp.arange(SOIL_TYPES, dtype=jnp.int32)
    one_hot = (soil_index[None] == soil_kinds[:, None, None]).astype(jnp.float32)
    ks = jnp.sum(one_hot * ks_table[:, None, None], axis=0)
    alpha = jnp.sum(one_hot * alpha_table[:, None, None], axis=0)
    return ks, alpha


def forecast(heads, soil_index, ks_table, alpha_table):
    members, rows, columns = heads.shape
    halo = MODEL_STEPS
    count = lax.axis_size("dev")
    me = lax.axis_index("dev")
    by_row = jnp.transpose(heads, (1, 0, 2))
    soil = soil_index.astype(jnp.float32)

    def edge(lo, hi):
        return jnp.concatenate([by_row[lo:hi].reshape(halo * members, columns), soil[lo:hi]], axis=0)

    above = lax.ppermute(edge(rows - halo, rows), "dev", [(i, i + 1) for i in range(count - 1)])
    below = lax.ppermute(edge(0, halo), "dev", [(i + 1, i) for i in range(count - 1)])

    def part(block):
        cut = halo * members
        return block[:cut].reshape(halo, members, columns), block[cut:]

    above_heads, above_soil = part(above)
    below_heads, below_soil = part(below)
    h = jnp.concatenate([above_heads, by_row, below_heads], axis=0)
    kinds = jnp.concatenate([above_soil, soil, below_soil], axis=0).astype(jnp.int32)
    ks, alpha = soil_values(kinds, ks_table, alpha_table)
    row = jnp.arange(rows + 2 * halo)
    inside = ((row >= halo) | (me > 0)) & ((row < rows + halo) | (me < count - 1))
    inside = inside.astype(jnp.float32)[:, None]
    ks = (ks * inside)[:, None, :]
    alpha = alpha[:, None, :]
    inside = inside[:, :, None]
    for _ in range(MODEL_STEPS):
        factor = jnp.exp(alpha * jnp.minimum(h, 0.0))
        k = ks * factor
        capacity = 0.1 + 0.4 * alpha * factor
        flux = 0.5 * (k[1:] + k[:-1]) * (h[1:] - h[:-1])
        mid, k_mid = h[1:-1], k[1:-1]
        vertical = 0.5 * (k_mid[..., 1:] + k_mid[..., :-1]) * (mid[..., 1:] - mid[..., :-1] - gravity_head)
        border = jnp.zeros_like(mid[..., :1])
        inflow = (
            flux[1:]
            - flux[:-1]
            + jnp.concatenate([vertical, border], -1)
            - jnp.concatenate([border, vertical], -1)
        )
        h = (mid + step_duration * inflow / capacity[1:-1]) * inside[1:-1]
        ks, alpha, inside = ks[1:-1], alpha[1:-1], inside[1:-1]
    return h


def total_over_devices(x):
    count = lax.axis_size("dev")
    groups = lax.axis_size("group")
    rows = x.shape[0] // 2
    core = lax.axis_index("dev") % 2
    other = [(i, i ^ 1) for i in range(count)]
    low, high = x[:rows], x[rows:]
    mine = jnp.where(core == 0, low, high)
    x = mine + lax.ppermute(jnp.where(core == 0, high, low), "dev", other)

    def turned(size, base, k, n):
        return [(i, i + (((i // base + k) % size) - (i // base) % size) * base) for i in range(n)]

    for axis, n, base, size in (
        ("dev", count, 2, 4),
        ("group", groups, 2, groups // 2),
        ("dev", count, 8, count // 8),
        ("group", groups, 1, 2),
    ):
        arrived = [lax.ppermute(x, axis, turned(size, base, k, n)) for k in range(1, size)]
        for a in arrived:
            x = x + a
    o = lax.ppermute(x, "dev", other)
    return jnp.concatenate([jnp.where(core == 0, x, o), jnp.where(core == 0, o, x)], axis=0)


def halves(x):
    high = x.astype(jnp.bfloat16)
    return high, (x - high.astype(jnp.float32)).astype(jnp.bfloat16)


def product(a, b, dims):
    (ah, al), (bh, bl) = a, b
    dot = lambda u, v: lax.dot_general(u, v, (dims, ((), ())), preferred_element_type=jnp.float32)
    return dot(ah, bh) + (dot(ah, bl) + dot(al, bh))


NN, NT, TN = ((1,), (0,)), ((1,), (1,)), ((0,), (0,))


def gram_kernel(mask_ref, heads_ref, op_ref, values_ref, spread_ref, packed_ref, joint_ref):
    sources, share, members, columns = heads_ref.shape
    total = sources * members
    lane = lax.broadcasted_iota(jnp.int32, (OBS, 256), 1)
    for r in range(share):
        acc = heads_ref[0, r]
        for s in range(1, sources):
            acc = acc + heads_ref[s, r]
        mean = jnp.sum(acc, axis=0, keepdims=True) / total
        parts = []
        for s in range(sources):
            part = heads_ref[s, r] - mean
            spread_ref[s, r] = part
            parts.append(part)
        parts.append(jnp.broadcast_to(mean, (8, columns)))
        rows = jnp.concatenate(parts, axis=0)
        for b in range(BLOCKS):
            at = r * BLOCKS + b
            high, low = halves(rows[:, 128 * b : 128 * b + 128])
            on = (mask_ref[r, b] != 0).astype(jnp.float32)
            op_high, op_low = halves(op_ref[at] * on)
            left = jnp.concatenate(
                [
                    jnp.concatenate([op_high, op_high], 1),
                    jnp.concatenate([op_low, jnp.zeros_like(op_low)], 1),
                ],
                0,
            )
            right = jnp.concatenate([high, low], 1)
            out = lax.dot_general(left, right, (NT, ((), ())), preferred_element_type=jnp.float32)
            out = out[:OBS] + out[OBS:]
            out = jnp.pad(out, ((0, 0), (0, 256 - out.shape[1])))
            innovation = values_ref[:, at : at + 1] * on - out
            joint = jnp.where(lane < total, out, jnp.where(lane == total, innovation, 0.0))
            joint_ref[OBS * at : OBS * at + OBS, :] = joint
    both = halves(joint_ref[...])
    gram = product(both, both, TN)
    side = lax.broadcasted_iota(jnp.int32, (64, 128), 1)
    packed_ref[0:64] = jnp.where(side < 64, gram[0:64, :128], gram[64:128, :128])
    packed_ref[64:128] = jnp.where(side < 64, gram[64:128, :128], pltpu.roll(gram[128:192, 128:], 64, 1))
    packed_ref[128:192] = gram[128:192, :128]
    packed_ref[192:200] = gram[192:200, :128]
    packed_ref[200:208] = gram[192:200, 128:]


def mean_and_gram(heads, op, mask, values):
    sources, share, members, columns = heads.shape
    anywhere = pl.BlockSpec(memory_space=pltpu.VMEM)
    return pl.pallas_call(
        gram_kernel,
        out_shape=(
            jax.ShapeDtypeStruct(heads.shape, jnp.float32),
            jax.ShapeDtypeStruct((208, 128), jnp.float32),
        ),
        in_specs=[pl.BlockSpec(memory_space=pltpu.SMEM), anywhere, anywhere, anywhere],
        out_specs=(anywhere, anywhere),
        scratch_shapes=[pltpu.VMEM((share * BLOCKS * OBS, 256), jnp.float32)],
        compiler_params=pltpu.CompilerParams(vmem_limit_bytes=40 * 2**20),
        name="gram",
    )(mask, heads, op, values)


def newton_kernel(packed_ref, out_ref, gram_ref):
    order = MEMBERS
    side = lax.broadcasted_iota(jnp.int32, (64, 128), 1)
    p0, p1, p2 = packed_ref[0:64], packed_ref[64:128], packed_ref[128:192]
    below = jnp.where(side < 64, p1, p0)
    turned = jnp.concatenate([p0, below], 0).T
    gram_ref[0:64, 0:128] = jnp.where(side < 64, p0, turned[0:64])
    gram_ref[64:128, 0:128] = below
    gram_ref[128:192, 0:128] = p2
    gram_ref[0:128, 128:192] = p2.T
    gram_ref[128:192, 128:192] = pltpu.roll(p1, 64, 1)[:, :64]
    eye = (
        lax.broadcasted_iota(jnp.int32, (order, order), 0)
        == lax.broadcasted_iota(jnp.int32, (order, order), 1)
    ).astype(jnp.float32)
    gram = gram_ref[...] + (MEMBERS - 1.0) * eye
    rhs = jnp.concatenate([packed_ref[192:200], packed_ref[200:208, :64]], 1)
    norm = jnp.sum(jnp.abs(gram), keepdims=True)
    inverse_norm = 1.0 / norm
    iterate = gram * inverse_norm
    middle = 1.5 * eye - 0.5 * iterate
    iterate = product(halves(iterate), halves(middle), NN)
    inverse = middle
    for step in range(1, NEWTON_STEPS):
        left = halves(inverse)
        middle = 1.5 * eye - 0.5 * product(left, halves(iterate), NN)
        right = halves(middle)
        if step < NEWTON_STEPS - 1:
            iterate = product(halves(iterate), right, NN)
        inverse = product(left, right, NN)
    final = halves(inverse)
    shift = product(halves(product(halves(rhs), final, NN)), final, NN) * inverse_norm
    out_ref[...] = jnp.sqrt((MEMBERS - 1.0) * inverse_norm) * inverse + shift[0:1]


def newton_weights(packed):
    return pl.pallas_call(
        newton_kernel,
        out_shape=jax.ShapeDtypeStruct((MEMBERS, MEMBERS), jnp.float32),
        in_specs=[pl.BlockSpec(memory_space=pltpu.VMEM)],
        out_specs=pl.BlockSpec(memory_space=pltpu.VMEM),
        scratch_shapes=[pltpu.VMEM((MEMBERS, MEMBERS), jnp.float32)],
        compiler_params=pltpu.CompilerParams(vmem_limit_bytes=40 * 2**20),
        name="newton",
    )(packed)


def mix_kernel(weights_ref, spread_ref, out_ref):
    sources, share, members, columns = spread_ref.shape
    weights = halves(weights_ref[...])
    for r in range(share):
        for c in range(0, columns, 256):
            s = jnp.concatenate([spread_ref[g, r, :, c : c + 256] for g in range(sources)], 0)
            mixed = product(weights, halves(s), NN)
            for g in range(sources):
                out_ref[g, r, :, c : c + 256] = mixed[members * g : members * g + members]


def mix(weights, spread):
    anywhere = pl.BlockSpec(memory_space=pltpu.VMEM)
    return pl.pallas_call(
        mix_kernel,
        out_shape=jax.ShapeDtypeStruct(spread.shape, jnp.float32),
        in_specs=[anywhere, anywhere],
        out_specs=anywhere,
        compiler_params=pltpu.CompilerParams(vmem_limit_bytes=40 * 2**20),
        name="mix",
    )(weights, spread)


def body(member_pressure_heads, soil_index, ks_table, alpha_table, obs_op, obs_mask, obs_values):
    predicted = forecast(member_pressure_heads, soil_index, ks_table, alpha_table)
    rows, members, columns = predicted.shape
    groups = lax.axis_size("group")
    share = rows // groups
    heads = lax.all_to_all(predicted.reshape(groups, share, members, columns), "group", 0, 0, tiled=True)
    op = obs_op.reshape(share * BLOCKS, OBS, 128)
    values = obs_values.reshape(share * BLOCKS, OBS).T
    spread, part = mean_and_gram(heads, op, obs_mask, values)
    mixed = mix(newton_weights(total_over_devices(part)), spread)
    back = lax.all_to_all(mixed, "group", 0, 0, tiled=True)
    return jnp.transpose(back.reshape(rows, members, columns), (1, 0, 2))


def solution(mesh):
    placed = (
        P("group", "dev", None),
        P("dev", None),
        P(),
        P(),
        P(("dev", "group"), None, None, None),
        P(("dev", "group"), None),
        P(("dev", "group"), None, None),
    )
    return jax.shard_map(
        body, mesh=mesh, in_specs=placed, out_specs=P("group", "dev", None), check_vma=False
    )
```

```python
import jax
import jax.numpy as jnp
from jax import lax
from jax.experimental import pallas as pl
from jax.experimental.pallas import tpu as pltpu
from jax.sharding import PartitionSpec as P

MEMBERS = 192
SOIL_TYPES = 8
MODEL_STEPS = 3
NEWTON_STEPS = 12
BLOCKS = 6
OBS = 32

HALO = MODEL_STEPS
LN2 = 0.6931471805599453
UNROLL = 4
EDGE_MIB = 60
gravity_head = 1.0
AXES = ("group", "dev")


def edges_kernel(ks_table, alpha_table, first_ref, last_ref, soil_ref, top_ref, bottom_ref, ks_ref, alpha_ref):
    members, span, columns = first_ref.shape
    rows = soil_ref.shape[0]
    ks, alpha = soil_tables(soil_ref[...], ks_table, alpha_table)
    ks_ref[...] = ks
    alpha_ref[...] = alpha
    flag = jnp.ones((8 - 2 * HALO, columns), jnp.float32)
    for j in range(HALO):
        top_ref[members * j : members * j + members] = first_ref[:, j, :]
        bottom_ref[members * j : members * j + members] = last_ref[:, span - HALO + j, :]
    top_ref[HALO * members :] = jnp.concatenate([ks[:HALO], alpha[:HALO], flag], 0)
    bottom_ref[HALO * members :] = jnp.concatenate([ks[rows - HALO :], alpha[rows - HALO :], flag], 0)


def law(h, ks, alpha, slope):
    factor = jnp.exp2(alpha * jnp.minimum(h, 0.0))
    return ks * factor, 1.0 / (1.0 + slope * factor)


def moved(h_ref, k_ref, gain_ref, low, count, members, inner):
    size = members * count
    around = slice(members * (low - 1), members * (low + count + 1))
    h_all, k_all = h_ref[around], k_ref[around]
    columns = h_all.shape[1]
    flux = (k_all[members:] + k_all[:-members]) * (h_all[members:] - h_all[:-members])
    h, k = h_all[members : members + size], k_all[members : members + size]
    face = (k + pltpu.roll(k, columns - 1, 1)) * ((pltpu.roll(h, columns - 1, 1) - gravity_head) - h)
    face = jnp.concatenate([face[:, : columns - 128], face[:, columns - 128 :] * inner], 1)
    gain = gain_ref[members * low : members * (low + count)]
    return h + gain * ((flux[members:] - flux[:size]) + (face - pltpu.roll(face, 1, 1)))


def soil_tables(kinds, ks_ref, alpha_ref):
    ks = jnp.zeros(kinds.shape, jnp.float32)
    alpha = jnp.zeros(kinds.shape, jnp.float32)
    for t in range(SOIL_TYPES):
        ks = jnp.where(kinds == t, 0.5 * ks_ref[t], ks)
        alpha = jnp.where(kinds == t, alpha_ref[t] / LN2, alpha)
    return ks, alpha


def rule(h, ks_ref, alpha_ref, low, count, members):
    def wide(rows):
        return jnp.concatenate([jnp.broadcast_to(x, (members, x.shape[1])) for x in rows], 0)

    alpha = [alpha_ref[r : r + 1] for r in range(low, low + count)]
    return law(
        h,
        wide([ks_ref[r : r + 1] for r in range(low, low + count)]),
        wide(alpha),
        wide([(4.0 * LN2) * x for x in alpha]),
    )


def inner_mask():
    return (lax.broadcasted_iota(jnp.int32, (1, 128), 1) < 127).astype(jnp.float32)


def interior_kernel(heads_ref, ks_ref, alpha_ref, out_ref, saved_ref, given, h0, h1, k0, k1, g0, g1, sems, in_sems, save_sems):
    members, rows, columns = given.shape
    tile = 8
    loads = [
        pltpu.make_async_copy(heads_ref.at[:, t : t + tile], given.at[:, t : t + tile], in_sems.at[t // tile])
        for t in range(0, rows, tile)
    ]
    for load in loads:
        load.start()
    inner = inner_mask()
    at = lambda r, n: slice(members * r, members * (r + n))
    for r in range(0, rows, 2):
        if r % tile == 0:
            loads[r // tile].wait()
        h = jnp.concatenate([given[:, r, :], given[:, r + 1, :]], 0)
        h0[at(r, 2)] = h
        k0[at(r, 2)], g0[at(r, 2)] = rule(h, ks_ref, alpha_ref, r, 2, members)
    now, later = (h0, k0, g0), (h1, k1, g1)
    copies = []

    def keep(ref, low, count, to):
        copies.append(pltpu.make_async_copy(ref.at[at(low, count)], saved_ref.at[at(to, count)], save_sems.at[len(copies)]))
        copies[-1].start()

    for step in range(1, MODEL_STEPS + 1):
        for low in range(step, rows - step, UNROLL):
            count = min(UNROLL, rows - step - low)
            h = moved(*now, low, count, members, inner)
            later[0][at(low, count)] = h
            if step < MODEL_STEPS:
                later[1][at(low, count)], later[2][at(low, count)] = rule(h, ks_ref, alpha_ref, low, count, members)
            else:
                for r in range(low, low + count):
                    copies.append(pltpu.make_async_copy(later[0].at[at(r, 1)], out_ref.at[r], sems.at[r]))
                    copies[-1].start()
        if step == 2:
            keep(h0, 0, 4, 0)
            keep(h0, rows - 4, 4, 4)
            keep(h1, 1, 2, 8)
            keep(h1, rows - 3, 2, 10)
        now, later = later, now
    for copy in copies:
        copy.wait()


def edge_kernel(above_ref, below_ref, saved_ref, own_ks, own_alpha, given_ref, out_ref, *scratch):
    del given_ref
    *states, ks_ref, alpha_ref, sems, in_sems = scratch
    rows, columns = own_ks.shape
    members = saved_ref.shape[0] // 12
    inner = inner_mask()
    cut = HALO * members
    at = lambda r, n: slice(members * r, members * (r + n))
    side = HALO + 4
    loads = []
    for step, (first, last) in enumerate(((0, 6), (8, 10), (2, 4))):
        for low, source in ((3, first), (5, last)):
            loads.append(
                pltpu.make_async_copy(saved_ref.at[at(source, 2)], states[3 * step].at[at(low, 2)], in_sems.at[len(loads)])
            )
            loads[-1].start()
    for n, ref, own in ((0, ks_ref, own_ks), (1, alpha_ref, own_alpha)):
        far = slice(cut + HALO * n, cut + HALO * n + HALO)
        ref[0:HALO] = above_ref[far]
        ref[HALO:side] = own[0:4]
        ref[side : side + 4] = own[rows - 4 :]
        ref[side + 4 : 2 * side] = below_ref[far]
    flag = slice(cut + 2 * HALO, cut + 2 * HALO + 1)
    has_above, has_below = above_ref[flag], below_ref[flag]

    def put(h, step, low, count):
        table = low + step if low < 5 else side + low - 5 + 2 - step
        k, g = rule(h, ks_ref, alpha_ref, table, count, members)
        states[3 * step + 1][at(low, count)] = k
        for j in range(count):
            row = g[members * j : members * (j + 1)]
            if table + j < HALO:
                row = row * has_above
            if table + j >= side + 4:
                row = row * has_below
            states[3 * step + 2][at(low + j, 1)] = row

    h = [states[3 * step] for step in range(MODEL_STEPS)]
    h[0][at(0, HALO)] = above_ref[0:cut]
    h[0][at(7, HALO)] = below_ref[0:cut]
    put(h[0][at(0, HALO)], 0, 0, HALO)
    put(h[0][at(7, HALO)], 0, 7, HALO)
    for step in range(MODEL_STEPS):
        for n, low in enumerate((3, 5)):
            loads[2 * step + n].wait()
            put(h[step][at(low, 2)], step, low, 2)
    copies = []
    for step in range(MODEL_STEPS):
        for low in (1, 6):
            new = moved(*states[3 * step : 3 * step + 3], low, HALO, members, inner)
            if step < MODEL_STEPS - 1:
                to = 0 if low == 1 else 7
                h[step + 1][at(to, HALO)] = new
                put(new, step + 1, to, HALO)
                continue
            row = 0 if low == 1 else rows - HALO
            h[0][at(low, HALO)] = new
            for j in range(HALO):
                copies.append(pltpu.make_async_copy(h[0].at[at(low + j, 1)], out_ref.at[row + j], sems.at[len(copies)]))
                copies[-1].start()
    for copy in copies:
        copy.wait()


def forecast(heads, soil_index, ks_table, alpha_table):
    members, rows, columns = heads.shape
    count = lax.axis_size("dev")
    scalars = pl.BlockSpec(memory_space=pltpu.SMEM)
    anywhere = pl.BlockSpec(memory_space=pl.ANY)
    whole = pl.BlockSpec(memory_space=pltpu.VMEM)
    table_spec = pl.BlockSpec((rows, columns), lambda i: (0, 0))
    edge_rows = HALO * members + 8
    edge = jax.ShapeDtypeStruct((edge_rows, columns), jnp.float32)
    table_shape = jax.ShapeDtypeStruct((rows, columns), jnp.float32)
    edge_spec = pl.BlockSpec((edge_rows, columns), lambda i: (0, 0))
    limit = lambda mib: pltpu.CompilerParams(vmem_limit_bytes=mib * 2**20)
    first = pl.BlockSpec((members, 8, columns), lambda i: (0, 0, 0))
    last = pl.BlockSpec((members, 8, columns), lambda i: (0, rows // 8 - 1, 0))
    top, bottom, ks, alpha = pl.pallas_call(
        edges_kernel,
        grid=(1,),
        out_shape=(edge, edge, table_shape, table_shape),
        in_specs=[scalars, scalars, first, last, table_spec],
        out_specs=(edge_spec, edge_spec, table_spec, table_spec),
        compiler_params=limit(60),
        name="edges",
    )(ks_table, alpha_table, heads, heads, soil_index)
    above = lax.ppermute(bottom, "dev", [(i, i + 1) for i in range(count - 1)])
    below = lax.ppermute(top, "dev", [(i + 1, i) for i in range(count - 1)])
    state = lambda r: pltpu.VMEM((r * members, columns), jnp.float32)
    by_row = jax.ShapeDtypeStruct((rows, members, columns), jnp.float32)
    inside, saved = pl.pallas_call(
        interior_kernel,
        grid=(1,),
        out_shape=(by_row, jax.ShapeDtypeStruct((12 * members, columns), jnp.float32)),
        in_specs=[anywhere, table_spec, table_spec],
        out_specs=(anywhere, anywhere),
        scratch_shapes=[pltpu.VMEM((members, rows, columns), jnp.float32)]
        + [state(rows)] * 6
        + [pltpu.SemaphoreType.DMA((rows,)), pltpu.SemaphoreType.DMA((rows // 8,)), pltpu.SemaphoreType.DMA((4,))],
        compiler_params=limit(60),
        cost_estimate=pl.CostEstimate(flops=60_000_000, bytes_accessed=5_000_000, transcendentals=4_000_000),
        name="interior",
    )(heads, ks, alpha)
    return pl.pallas_call(
        edge_kernel,
        out_shape=by_row,
        in_specs=[whole, whole, anywhere, whole, whole, anywhere],
        out_specs=anywhere,
        scratch_shapes=[state(10)] * (3 * MODEL_STEPS)
        + [pltpu.VMEM((2 * (HALO + 4), columns), jnp.float32)] * 2
        + [pltpu.SemaphoreType.DMA((2 * HALO,))] * 2,
        input_output_aliases={5: 0},
        compiler_params=limit(EDGE_MIB),
        name="edge",
    )(above, below, saved, ks, alpha, inside)


def along_z(k):
    groups, count = lax.axis_size("group"), lax.axis_size("dev")
    top = count // 2
    pairs = []
    for g in range(groups):
        for d in range(count):
            z = (2 * (d // top) + g % 2 + k) % 4
            pairs.append((g * count + d, (g // 2 * 2 + z % 2) * count + z // 2 * top + d % top))
    return pairs


def total_over_devices(x):
    count = lax.axis_size("dev")
    groups = lax.axis_size("group")
    rows = x.shape[0] // 2
    core = lax.axis_index("dev") % 2
    other = [(i, i ^ 1) for i in range(count)]
    low, high = x[:rows], x[rows:]
    mine = jnp.where(core == 0, low, high)
    x = mine + lax.ppermute(jnp.where(core == 0, high, low), "dev", other)

    def turned(size, base, k, n):
        if base == 0:
            return along_z(k)
        return [(i, i + (((i // base + k) % size) - (i // base) % size) * base) for i in range(n)]

    for axis, n, base, size in (
        ("dev", count, 2, 4),
        ("group", groups, 2, groups // 2),
        (AXES, groups * count, 0, 4),
    ):
        arrived = [lax.ppermute(x, axis, turned(size, base, k, n)) for k in range(1, size)]
        for a in arrived:
            x = x + a
    o = lax.ppermute(x, "dev", other)
    return jnp.concatenate([jnp.where(core == 0, x, o), jnp.where(core == 0, o, x)], axis=0)


def halves(x):
    high = x.astype(jnp.bfloat16)
    return high, (x - high.astype(jnp.float32)).astype(jnp.bfloat16)


def product(a, b, dims):
    (ah, al), (bh, bl) = a, b
    dot = lambda u, v: lax.dot_general(u, v, (dims, ((), ())), preferred_element_type=jnp.float32)
    return dot(ah, bh) + (dot(ah, bl) + dot(al, bh))


NN, NT, TN = ((1,), (0,)), ((1,), (1,)), ((0,), (0,))


def gram_kernel(mask_ref, op_ref, values_ref, heads_ref, spread_ref, packed_ref, joint_ref):
    sources, share, members, columns = spread_ref.shape
    total = sources * members
    lane = lax.broadcasted_iota(jnp.int32, (OBS, 256), 1)
    for r in range(share):
        whole = [heads_ref[s, r] for s in range(sources)]
        acc = whole[0]
        for s in range(1, sources):
            acc = acc + whole[s]
        mean = jnp.sum(acc, axis=0, keepdims=True) / total
        parts = []
        for s in range(sources):
            part = whole[s] - mean
            spread_ref[s, r] = part
            parts.append(part)
        parts.append(jnp.broadcast_to(mean, (8, columns)))
        rows = jnp.concatenate(parts, axis=0)
        for b in range(BLOCKS):
            at = r * BLOCKS + b
            high, low = halves(rows[:, 128 * b : 128 * b + 128])
            on = (mask_ref[r, b] != 0).astype(jnp.float32)
            op_high, op_low = halves(op_ref[at] * on)
            left = jnp.concatenate(
                [
                    jnp.concatenate([op_high, op_high], 1),
                    jnp.concatenate([op_low, jnp.zeros_like(op_low)], 1),
                ],
                0,
            )
            right = jnp.concatenate([high, low], 1)
            out = lax.dot_general(left, right, (NT, ((), ())), preferred_element_type=jnp.float32)
            out = out[:OBS] + out[OBS:]
            out = jnp.pad(out, ((0, 0), (0, 256 - out.shape[1])))
            innovation = values_ref[:, at : at + 1] * on - out
            joint = jnp.where(lane < total, out, jnp.where(lane == total, innovation, 0.0))
            joint_ref[OBS * at : OBS * at + OBS, :] = joint
    both = halves(joint_ref[...])
    gram = product(both, both, TN)
    side = lax.broadcasted_iota(jnp.int32, (64, 128), 1)
    packed_ref[0:64] = jnp.where(side < 64, gram[0:64, :128], gram[64:128, :128])
    packed_ref[64:128] = jnp.where(side < 64, gram[64:128, :128], pltpu.roll(gram[128:192, 128:], 64, 1))
    packed_ref[128:192] = gram[128:192, :128]
    packed_ref[192:200] = gram[192:200, :128]
    packed_ref[200:208] = gram[192:200, 128:]


def mean_and_gram(heads, op, mask, values):
    sources, share, members, columns = heads.shape
    anywhere = pl.BlockSpec(memory_space=pltpu.VMEM)
    return pl.pallas_call(
        gram_kernel,
        out_shape=(
            jax.ShapeDtypeStruct(heads.shape, jnp.float32),
            jax.ShapeDtypeStruct((208, 128), jnp.float32),
        ),
        in_specs=[pl.BlockSpec(memory_space=pltpu.SMEM), anywhere, anywhere] + [anywhere],
        out_specs=(anywhere, anywhere),
        scratch_shapes=[pltpu.VMEM((share * BLOCKS * OBS, 256), jnp.float32)],
        compiler_params=pltpu.CompilerParams(vmem_limit_bytes=40 * 2**20),
        name="gram",
    )(mask, op, values, heads)


def newton_kernel(packed_ref, out_ref, gram_ref):
    order = MEMBERS
    side = lax.broadcasted_iota(jnp.int32, (64, 128), 1)
    p0, p1, p2 = packed_ref[0:64], packed_ref[64:128], packed_ref[128:192]
    below = jnp.where(side < 64, p1, p0)
    turned = jnp.concatenate([p0, below], 0).T
    gram_ref[0:64, 0:128] = jnp.where(side < 64, p0, turned[0:64])
    gram_ref[64:128, 0:128] = below
    gram_ref[128:192, 0:128] = p2
    gram_ref[0:128, 128:192] = p2.T
    gram_ref[128:192, 128:192] = pltpu.roll(p1, 64, 1)[:, :64]
    eye = (
        lax.broadcasted_iota(jnp.int32, (order, order), 0)
        == lax.broadcasted_iota(jnp.int32, (order, order), 1)
    ).astype(jnp.float32)
    gram = gram_ref[...] + (MEMBERS - 1.0) * eye
    rhs = jnp.concatenate([packed_ref[192:200], packed_ref[200:208, :64]], 1)
    norm = jnp.sum(jnp.abs(gram), keepdims=True)
    inverse_norm = 1.0 / norm
    iterate = gram * inverse_norm
    middle = 1.5 * eye - 0.5 * iterate
    iterate = product(halves(iterate), halves(middle), NN)
    inverse = middle
    for step in range(1, NEWTON_STEPS):
        left = halves(inverse)
        middle = 1.5 * eye - 0.5 * product(left, halves(iterate), NN)
        right = halves(middle)
        if step < NEWTON_STEPS - 1:
            iterate = product(halves(iterate), right, NN)
        inverse = product(left, right, NN)
    final = halves(inverse)
    shift = product(halves(product(halves(rhs), final, NN)), final, NN) * inverse_norm
    out_ref[...] = jnp.sqrt((MEMBERS - 1.0) * inverse_norm) * inverse + shift[0:1]


def newton_weights(packed):
    return pl.pallas_call(
        newton_kernel,
        out_shape=jax.ShapeDtypeStruct((MEMBERS, MEMBERS), jnp.float32),
        in_specs=[pl.BlockSpec(memory_space=pltpu.VMEM)],
        out_specs=pl.BlockSpec(memory_space=pltpu.VMEM),
        scratch_shapes=[pltpu.VMEM((MEMBERS, MEMBERS), jnp.float32)],
        compiler_params=pltpu.CompilerParams(vmem_limit_bytes=40 * 2**20),
        name="newton",
    )(packed)


def mix_kernel(weights_ref, spread_ref, out_ref):
    sources, share, members, columns = spread_ref.shape
    weights = halves(weights_ref[...])
    for r in range(share):
        for c in range(0, columns, 256):
            s = jnp.concatenate([spread_ref[g, r, :, c : c + 256] for g in range(sources)], 0)
            mixed = product(weights, halves(s), NN)
            for g in range(sources):
                out_ref[g, r, :, c : c + 256] = mixed[members * g : members * g + members]


def mix(weights, spread):
    anywhere = pl.BlockSpec(memory_space=pltpu.VMEM)
    return pl.pallas_call(
        mix_kernel,
        out_shape=jax.ShapeDtypeStruct(spread.shape, jnp.float32),
        in_specs=[anywhere, anywhere],
        out_specs=anywhere,
        compiler_params=pltpu.CompilerParams(vmem_limit_bytes=40 * 2**20),
        name="mix",
    )(weights, spread)


def body(member_pressure_heads, soil_index, ks_table, alpha_table, obs_op, obs_mask, obs_values):
    members, rows, columns = member_pressure_heads.shape
    groups = lax.axis_size("group")
    share = rows // groups
    predicted = forecast(member_pressure_heads, soil_index, ks_table, alpha_table)
    heads = lax.all_to_all(predicted.reshape(groups, share, members, columns), "group", 0, 0, tiled=True)
    op = obs_op.reshape(share * BLOCKS, OBS, 128)
    values = obs_values.reshape(share * BLOCKS, OBS).T
    spread, part = mean_and_gram(heads, op, obs_mask, values)
    mixed = mix(newton_weights(total_over_devices(part)), spread)
    back = lax.all_to_all(mixed, "group", 0, 0, tiled=True)
    return jnp.transpose(back.reshape(rows, members, columns), (1, 0, 2))


def solution(mesh):
    placed = (
        P("group", "dev", None),
        P("dev", None),
        P(),
        P(),
        P(("dev", "group"), None, None, None),
        P(("dev", "group"), None),
        P(("dev", "group"), None, None),
    )
    return jax.shard_map(
        body, mesh=mesh, in_specs=placed, out_specs=P("group", "dev", None), check_vma=False
    )
```

```python
import jax
import jax.numpy as jnp
from jax import lax
from jax.experimental import pallas as pl
from jax.experimental.pallas import tpu as pltpu
from jax.sharding import PartitionSpec as P

MEMBERS = 192
SOIL_TYPES = 8
MODEL_STEPS = 3
NEWTON_STEPS = 12
BLOCKS = 6
OBS = 32

HALO = MODEL_STEPS
LN2 = 0.6931471805599453
UNROLL = 4
FORECAST_MIB = 32
gravity_head = 1.0
AXES = ("group", "dev")


def edges_kernel(ks_far, alpha_far, heads_ref, soil_far, top_ref, bottom_ref, tables_ref, ks_table, alpha_table, soil_ref, first, last, sems):
    members, span, columns = first.shape
    rows = soil_ref.shape[0]
    loads = [
        pltpu.make_async_copy(source, ref, sems.at[n])
        for n, (source, ref) in enumerate(
            (
                (ks_far, ks_table),
                (alpha_far, alpha_table),
                (soil_far, soil_ref),
                (heads_ref.at[:, 0:span], first),
                (heads_ref.at[:, rows - span : rows], last),
            )
        )
    ]
    for load in loads:
        load.start()
    for load in loads[:3]:
        load.wait()
    ks, alpha = soil_tables(soil_ref[...], ks_table, alpha_table)
    tables_ref[0:rows] = ks
    tables_ref[rows:] = alpha
    flag = jnp.ones((8 - 2 * HALO, columns), jnp.float32)
    top_ref[HALO * members :] = jnp.concatenate([ks[:HALO], alpha[:HALO], flag], 0)
    bottom_ref[HALO * members :] = jnp.concatenate([ks[rows - HALO :], alpha[rows - HALO :], flag], 0)
    for load in loads[3:]:
        load.wait()
    for j in range(HALO):
        top_ref[members * j : members * j + members] = first[:, j, :]
        bottom_ref[members * j : members * j + members] = last[:, span - HALO + j, :]


def law(h, ks, alpha, slope):
    factor = jnp.exp2(alpha * jnp.minimum(h, 0.0))
    return ks * factor, 1.0 / (1.0 + slope * factor)


def moved(h_ref, k_ref, gain_ref, low, count, members, inner):
    size = members * count
    around = slice(members * (low - 1), members * (low + count + 1))
    h_all, k_all = h_ref[around], k_ref[around]
    columns = h_all.shape[1]
    flux = (k_all[members:] + k_all[:-members]) * (h_all[members:] - h_all[:-members])
    h, k = h_all[members : members + size], k_all[members : members + size]
    face = (k + pltpu.roll(k, columns - 1, 1)) * ((pltpu.roll(h, columns - 1, 1) - gravity_head) - h)
    face = jnp.concatenate([face[:, : columns - 128], face[:, columns - 128 :] * inner], 1)
    gain = gain_ref[members * low : members * (low + count)]
    return h + gain * ((flux[members:] - flux[:size]) + (face - pltpu.roll(face, 1, 1)))


def soil_tables(kinds, ks_ref, alpha_ref):
    ks = jnp.zeros(kinds.shape, jnp.float32)
    alpha = jnp.zeros(kinds.shape, jnp.float32)
    for t in range(SOIL_TYPES):
        ks = jnp.where(kinds == t, 0.5 * ks_ref[t], ks)
        alpha = jnp.where(kinds == t, alpha_ref[t] / LN2, alpha)
    return ks, alpha


def rule(h, ks_ref, alpha_ref, low, count, members):
    def wide(rows):
        return jnp.concatenate([jnp.broadcast_to(x, (members, x.shape[1])) for x in rows], 0)

    alpha = [alpha_ref[r : r + 1] for r in range(low, low + count)]
    return law(
        h,
        wide([ks_ref[r : r + 1] for r in range(low, low + count)]),
        wide(alpha),
        wide([(4.0 * LN2) * x for x in alpha]),
    )


def inner_mask():
    return (lax.broadcasted_iota(jnp.int32, (1, 128), 1) < 127).astype(jnp.float32)


def interior_kernel(heads_ref, tables_ref, out_ref, saved_ref, given, h0, h1, k0, k1, g0, g1, sems, in_sems, save_sems):
    members, rows, columns = given.shape
    ks_ref, alpha_ref = tables_ref.at[0:rows], tables_ref.at[rows:]
    tile = 8
    loads = [
        pltpu.make_async_copy(heads_ref.at[:, t : t + tile], given.at[:, t : t + tile], in_sems.at[t // tile])
        for t in range(0, rows, tile)
    ]
    for load in loads:
        load.start()
    inner = inner_mask()
    at = lambda r, n: slice(members * r, members * (r + n))
    for r in range(0, rows, 2):
        if r % tile == 0:
            loads[r // tile].wait()
        h = jnp.concatenate([given[:, r, :], given[:, r + 1, :]], 0)
        h0[at(r, 2)] = h
        k0[at(r, 2)], g0[at(r, 2)] = rule(h, ks_ref, alpha_ref, r, 2, members)
    now, later = (h0, k0, g0), (h1, k1, g1)
    copies = []

    def keep(ref, low, count, to):
        copies.append(pltpu.make_async_copy(ref.at[at(low, count)], saved_ref.at[at(to, count)], save_sems.at[len(copies)]))
        copies[-1].start()

    for step in range(1, MODEL_STEPS + 1):
        for low in range(step, rows - step, UNROLL):
            count = min(UNROLL, rows - step - low)
            h = moved(*now, low, count, members, inner)
            later[0][at(low, count)] = h
            if step < MODEL_STEPS:
                later[1][at(low, count)], later[2][at(low, count)] = rule(h, ks_ref, alpha_ref, low, count, members)
            else:
                for r in range(low, low + count):
                    copies.append(pltpu.make_async_copy(later[0].at[at(r, 1)], out_ref.at[r], sems.at[r]))
                    copies[-1].start()
        if step == 2:
            keep(h0, 0, 4, 0)
            keep(h0, rows - 4, 4, 4)
            keep(h1, 1, 2, 8)
            keep(h1, rows - 3, 2, 10)
        now, later = later, now
    for copy in copies:
        copy.wait()


def edge_kernel(above_ref, below_ref, saved_ref, tables_ref, given_ref, out_ref, *scratch):
    del given_ref
    *states, ks_ref, alpha_ref, sems = scratch
    rows = tables_ref.shape[0] // 2
    members = saved_ref.shape[0] // 12
    inner = inner_mask()
    cut = HALO * members
    at = lambda r, n: slice(members * r, members * (r + n))
    side = HALO + 4
    for n, ref in ((0, ks_ref), (1, alpha_ref)):
        far = slice(cut + HALO * n, cut + HALO * n + HALO)
        ref[0:HALO] = above_ref[far]
        ref[HALO:side] = tables_ref[rows * n : rows * n + 4]
        ref[side : side + 4] = tables_ref[rows * n + rows - 4 : rows * n + rows]
        ref[side + 4 : 2 * side] = below_ref[far]
    flag = slice(cut + 2 * HALO, cut + 2 * HALO + 1)
    has_above, has_below = above_ref[flag], below_ref[flag]

    def put(h, step, low, count):
        table = low + step if low < 5 else side + low - 5 + 2 - step
        k, g = rule(h, ks_ref, alpha_ref, table, count, members)
        states[3 * step + 1][at(low, count)] = k
        for j in range(count):
            row = g[members * j : members * (j + 1)]
            if table + j < HALO:
                row = row * has_above
            if table + j >= side + 4:
                row = row * has_below
            states[3 * step + 2][at(low + j, 1)] = row

    h = [states[3 * step] for step in range(MODEL_STEPS)]
    h[0][at(0, HALO)] = above_ref[0:cut]
    h[0][at(7, HALO)] = below_ref[0:cut]
    put(h[0][at(0, HALO)], 0, 0, HALO)
    put(h[0][at(7, HALO)], 0, 7, HALO)
    for step in range(MODEL_STEPS):
        for low, source in zip((3, 5), ((0, 6), (8, 10), (2, 4))[step]):
            kept = saved_ref[at(source, 2)]
            h[step][at(low, 2)] = kept
            put(kept, step, low, 2)
    copies = []
    for step in range(MODEL_STEPS):
        for low in (1, 6):
            new = moved(*states[3 * step : 3 * step + 3], low, HALO, members, inner)
            if step < MODEL_STEPS - 1:
                to = 0 if low == 1 else 7
                h[step + 1][at(to, HALO)] = new
                put(new, step + 1, to, HALO)
                continue
            row = 0 if low == 1 else rows - HALO
            h[0][at(low, HALO)] = new
            for j in range(HALO):
                copies.append(pltpu.make_async_copy(h[0].at[at(low + j, 1)], out_ref.at[row + j], sems.at[len(copies)]))
                copies[-1].start()
    for copy in copies:
        copy.wait()


def forecast(heads, soil_index, ks_table, alpha_table):
    members, rows, columns = heads.shape
    count = lax.axis_size("dev")
    far = pl.BlockSpec(memory_space=pltpu.HBM)
    near = pl.BlockSpec(memory_space=pltpu.VMEM)
    edge = jax.ShapeDtypeStruct((HALO * members + 8, columns), jnp.float32)
    table = jax.ShapeDtypeStruct((2 * rows, columns), jnp.float32)
    block = pltpu.VMEM((members, 8, columns), jnp.float32)
    limit = lambda mib: pltpu.CompilerParams(vmem_limit_bytes=mib * 2**20)
    top, bottom, tables = pl.pallas_call(
        edges_kernel,
        out_shape=(edge, edge, table),
        in_specs=[far] * 4,
        out_specs=(near, near, near),
        scratch_shapes=[pltpu.SMEM((SOIL_TYPES,), jnp.float32)] * 2
        + [pltpu.VMEM((rows, columns), jnp.int32), block, block, pltpu.SemaphoreType.DMA((5,))],
        compiler_params=limit(60),
        name="edges",
    )(ks_table, alpha_table, heads, soil_index)
    above = lax.ppermute(bottom, "dev", [(i, i + 1) for i in range(count - 1)])
    below = lax.ppermute(top, "dev", [(i + 1, i) for i in range(count - 1)])
    state = lambda r: pltpu.VMEM((r * members, columns), jnp.float32)
    by_row = jax.ShapeDtypeStruct((rows, members, columns), jnp.float32)
    inside, saved = pl.pallas_call(
        interior_kernel,
        out_shape=(by_row, jax.ShapeDtypeStruct((12 * members, columns), jnp.float32)),
        in_specs=[far, near],
        out_specs=(far, near),
        scratch_shapes=[pltpu.VMEM((members, rows, columns), jnp.float32)]
        + [state(rows)] * 6
        + [pltpu.SemaphoreType.DMA((rows,)), pltpu.SemaphoreType.DMA((rows // 8,)), pltpu.SemaphoreType.DMA((4,))],
        compiler_params=limit(FORECAST_MIB),
        cost_estimate=pl.CostEstimate(flops=60_000_000, bytes_accessed=5_000_000, transcendentals=4_000_000),
        name="interior",
    )(heads, tables)
    return pl.pallas_call(
        edge_kernel,
        out_shape=by_row,
        in_specs=[near] * 4 + [far],
        out_specs=far,
        scratch_shapes=[state(10)] * (3 * MODEL_STEPS)
        + [pltpu.VMEM((2 * (HALO + 4), columns), jnp.float32)] * 2
        + [pltpu.SemaphoreType.DMA((2 * HALO,))],
        input_output_aliases={4: 0},
        compiler_params=limit(FORECAST_MIB),
        name="edge",
    )(above, below, saved, tables, inside)


def along_z(k):
    groups, count = lax.axis_size("group"), lax.axis_size("dev")
    top = count // 2
    pairs = []
    for g in range(groups):
        for d in range(count):
            z = (2 * (d // top) + g % 2 + k) % 4
            pairs.append((g * count + d, (g // 2 * 2 + z % 2) * count + z // 2 * top + d % top))
    return pairs


def total_over_devices(x):
    count = lax.axis_size("dev")
    groups = lax.axis_size("group")
    rows = x.shape[0] // 2
    core = lax.axis_index("dev") % 2
    other = [(i, i ^ 1) for i in range(count)]
    low, high = x[:rows], x[rows:]
    mine = jnp.where(core == 0, low, high)
    x = mine + lax.ppermute(jnp.where(core == 0, high, low), "dev", other)

    def turned(size, base, k, n):
        if base == 0:
            return along_z(k)
        return [(i, i + (((i // base + k) % size) - (i // base) % size) * base) for i in range(n)]

    for axis, n, base, size in (
        ("dev", count, 2, 4),
        ("group", groups, 2, groups // 2),
        (AXES, groups * count, 0, 4),
    ):
        arrived = [lax.ppermute(x, axis, turned(size, base, k, n)) for k in range(1, size)]
        for a in arrived:
            x = x + a
    o = lax.ppermute(x, "dev", other)
    return jnp.concatenate([jnp.where(core == 0, x, o), jnp.where(core == 0, o, x)], axis=0)


def halves(x):
    high = x.astype(jnp.bfloat16)
    return high, (x - high.astype(jnp.float32)).astype(jnp.bfloat16)


def product(a, b, dims):
    (ah, al), (bh, bl) = a, b
    dot = lambda u, v: lax.dot_general(u, v, (dims, ((), ())), preferred_element_type=jnp.float32)
    return dot(ah, bh) + (dot(ah, bl) + dot(al, bh))


NN, NT, TN = ((1,), (0,)), ((1,), (1,)), ((0,), (0,))


def gram_kernel(mask_ref, op_ref, values_ref, heads_ref, spread_ref, packed_ref, joint_ref):
    sources, share, members, columns = spread_ref.shape
    total = sources * members
    lane = lax.broadcasted_iota(jnp.int32, (OBS, 256), 1)
    for r in range(share):
        whole = [heads_ref[s, r] for s in range(sources)]
        acc = whole[0]
        for s in range(1, sources):
            acc = acc + whole[s]
        mean = jnp.sum(acc, axis=0, keepdims=True) / total
        parts = []
        for s in range(sources):
            part = whole[s] - mean
            spread_ref[s, r] = part
            parts.append(part)
        parts.append(jnp.broadcast_to(mean, (8, columns)))
        rows = jnp.concatenate(parts, axis=0)
        for b in range(BLOCKS):
            at = r * BLOCKS + b
            high, low = halves(rows[:, 128 * b : 128 * b + 128])
            on = (mask_ref[r, b] != 0).astype(jnp.float32)
            op_high, op_low = halves(op_ref[at] * on)
            left = jnp.concatenate(
                [
                    jnp.concatenate([op_high, op_high], 1),
                    jnp.concatenate([op_low, jnp.zeros_like(op_low)], 1),
                ],
                0,
            )
            right = jnp.concatenate([high, low], 1)
            out = lax.dot_general(left, right, (NT, ((), ())), preferred_element_type=jnp.float32)
            out = out[:OBS] + out[OBS:]
            out = jnp.pad(out, ((0, 0), (0, 256 - out.shape[1])))
            innovation = values_ref[:, at : at + 1] * on - out
            joint = jnp.where(lane < total, out, jnp.where(lane == total, innovation, 0.0))
            joint_ref[OBS * at : OBS * at + OBS, :] = joint
    both = halves(joint_ref[...])
    gram = product(both, both, TN)
    side = lax.broadcasted_iota(jnp.int32, (64, 128), 1)
    packed_ref[0:64] = jnp.where(side < 64, gram[0:64, :128], gram[64:128, :128])
    packed_ref[64:128] = jnp.where(side < 64, gram[64:128, :128], pltpu.roll(gram[128:192, 128:], 64, 1))
    packed_ref[128:192] = gram[128:192, :128]
    packed_ref[192:200] = gram[192:200, :128]
    packed_ref[200:208] = gram[192:200, 128:]


def mean_and_gram(heads, op, mask, values):
    sources, share, members, columns = heads.shape
    anywhere = pl.BlockSpec(memory_space=pltpu.VMEM)
    return pl.pallas_call(
        gram_kernel,
        out_shape=(
            jax.ShapeDtypeStruct(heads.shape, jnp.float32),
            jax.ShapeDtypeStruct((208, 128), jnp.float32),
        ),
        in_specs=[pl.BlockSpec(memory_space=pltpu.SMEM), anywhere, anywhere] + [anywhere],
        out_specs=(anywhere, anywhere),
        scratch_shapes=[pltpu.VMEM((share * BLOCKS * OBS, 256), jnp.float32)],
        compiler_params=pltpu.CompilerParams(vmem_limit_bytes=40 * 2**20),
        name="gram",
    )(mask, op, values, heads)


def newton_kernel(packed_ref, out_ref, gram_ref):
    order = MEMBERS
    side = lax.broadcasted_iota(jnp.int32, (64, 128), 1)
    p0, p1, p2 = packed_ref[0:64], packed_ref[64:128], packed_ref[128:192]
    below = jnp.where(side < 64, p1, p0)
    turned = jnp.concatenate([p0, below], 0).T
    gram_ref[0:64, 0:128] = jnp.where(side < 64, p0, turned[0:64])
    gram_ref[64:128, 0:128] = below
    gram_ref[128:192, 0:128] = p2
    gram_ref[0:128, 128:192] = p2.T
    gram_ref[128:192, 128:192] = pltpu.roll(p1, 64, 1)[:, :64]
    eye = (
        lax.broadcasted_iota(jnp.int32, (order, order), 0)
        == lax.broadcasted_iota(jnp.int32, (order, order), 1)
    ).astype(jnp.float32)
    gram = gram_ref[...] + (MEMBERS - 1.0) * eye
    rhs = jnp.concatenate([packed_ref[192:200], packed_ref[200:208, :64]], 1)
    norm = jnp.sum(jnp.abs(gram), keepdims=True)
    inverse_norm = 1.0 / norm
    iterate = gram * inverse_norm
    middle = 1.5 * eye - 0.5 * iterate
    iterate = product(halves(iterate), halves(middle), NN)
    inverse = middle
    for step in range(1, NEWTON_STEPS):
        left = halves(inverse)
        middle = 1.5 * eye - 0.5 * product(left, halves(iterate), NN)
        right = halves(middle)
        if step < NEWTON_STEPS - 1:
            iterate = product(halves(iterate), right, NN)
        inverse = product(left, right, NN)
    final = halves(inverse)
    shift = product(halves(product(halves(rhs), final, NN)), final, NN) * inverse_norm
    out_ref[...] = jnp.sqrt((MEMBERS - 1.0) * inverse_norm) * inverse + shift[0:1]


def newton_weights(packed):
    return pl.pallas_call(
        newton_kernel,
        out_shape=jax.ShapeDtypeStruct((MEMBERS, MEMBERS), jnp.float32),
        in_specs=[pl.BlockSpec(memory_space=pltpu.VMEM)],
        out_specs=pl.BlockSpec(memory_space=pltpu.VMEM),
        scratch_shapes=[pltpu.VMEM((MEMBERS, MEMBERS), jnp.float32)],
        compiler_params=pltpu.CompilerParams(vmem_limit_bytes=40 * 2**20),
        name="newton",
    )(packed)


def mix_kernel(weights_ref, spread_ref, out_ref):
    sources, share, members, columns = spread_ref.shape
    weights = halves(weights_ref[...])
    for r in range(share):
        for c in range(0, columns, 256):
            s = jnp.concatenate([spread_ref[g, r, :, c : c + 256] for g in range(sources)], 0)
            mixed = product(weights, halves(s), NN)
            for g in range(sources):
                out_ref[g, r, :, c : c + 256] = mixed[members * g : members * g + members]


def mix(weights, spread):
    anywhere = pl.BlockSpec(memory_space=pltpu.VMEM)
    return pl.pallas_call(
        mix_kernel,
        out_shape=jax.ShapeDtypeStruct(spread.shape, jnp.float32),
        in_specs=[anywhere, anywhere],
        out_specs=anywhere,
        compiler_params=pltpu.CompilerParams(vmem_limit_bytes=40 * 2**20),
        name="mix",
    )(weights, spread)


def body(member_pressure_heads, soil_index, ks_table, alpha_table, obs_op, obs_mask, obs_values):
    members, rows, columns = member_pressure_heads.shape
    groups = lax.axis_size("group")
    share = rows // groups
    predicted = forecast(member_pressure_heads, soil_index, ks_table, alpha_table)
    heads = lax.all_to_all(predicted.reshape(groups, share, members, columns), "group", 0, 0, tiled=True)
    op = obs_op.reshape(share * BLOCKS, OBS, 128)
    values = obs_values.reshape(share * BLOCKS, OBS).T
    spread, part = mean_and_gram(heads, op, obs_mask, values)
    mixed = mix(newton_weights(total_over_devices(part)), spread)
    back = lax.all_to_all(mixed, "group", 0, 0, tiled=True)
    return jnp.transpose(back.reshape(rows, members, columns), (1, 0, 2))


def solution(mesh):
    placed = (
        P("group", "dev", None),
        P("dev", None),
        P(),
        P(),
        P(("dev", "group"), None, None, None),
        P(("dev", "group"), None),
        P(("dev", "group"), None, None),
    )
    return jax.shard_map(
        body, mesh=mesh, in_specs=placed, out_specs=P("group", "dev", None), check_vma=False
    )
```

```python
import jax
import jax.numpy as jnp
from jax import lax
from jax.experimental import pallas as pl
from jax.experimental.pallas import tpu as pltpu
from jax.sharding import PartitionSpec as P

MEMBERS = 192
SOIL_TYPES = 8
MODEL_STEPS = 3
NEWTON_STEPS = 12
BLOCKS = 6
OBS = 32

HALO = MODEL_STEPS
LN2 = 0.6931471805599453
UNROLL = 4
FORECAST_MIB = 32
gravity_head = 1.0
AXES = ("group", "dev")


def edges_kernel(ks_far, alpha_far, heads_ref, soil_far, top_ref, bottom_ref, tables_ref, ks_table, alpha_table, soil_ref, first, last, sems):
    members, span, columns = first.shape
    rows = soil_ref.shape[0]
    loads = [
        pltpu.make_async_copy(source, ref, sems.at[n])
        for n, (source, ref) in enumerate(
            (
                (ks_far, ks_table),
                (alpha_far, alpha_table),
                (soil_far, soil_ref),
                (heads_ref.at[:, 0:span], first),
                (heads_ref.at[:, rows - span : rows], last),
            )
        )
    ]
    for load in loads:
        load.start()
    for load in loads[:3]:
        load.wait()
    ks, alpha = soil_tables(soil_ref[...], ks_table, alpha_table)
    tables_ref[0:rows] = ks
    tables_ref[rows:] = alpha
    flag = jnp.ones((8 - 2 * HALO, columns), jnp.float32)
    top_ref[HALO * members :] = jnp.concatenate([ks[:HALO], alpha[:HALO], flag], 0)
    bottom_ref[HALO * members :] = jnp.concatenate([ks[rows - HALO :], alpha[rows - HALO :], flag], 0)
    for load in loads[3:]:
        load.wait()
    for j in range(HALO):
        top_ref[members * j : members * j + members] = first[:, j, :]
        bottom_ref[members * j : members * j + members] = last[:, span - HALO + j, :]


def law(h, ks, alpha, slope):
    factor = jnp.exp2(alpha * jnp.minimum(h, 0.0))
    return ks * factor, 1.0 / (1.0 + slope * factor)


def moved(h_ref, k_ref, gain_ref, low, count, members, inner):
    size = members * count
    around = slice(members * (low - 1), members * (low + count + 1))
    h_all, k_all = h_ref[around], k_ref[around]
    columns = h_all.shape[1]
    flux = (k_all[members:] + k_all[:-members]) * (h_all[members:] - h_all[:-members])
    h, k = h_all[members : members + size], k_all[members : members + size]
    face = (k + pltpu.roll(k, columns - 1, 1)) * ((pltpu.roll(h, columns - 1, 1) - gravity_head) - h)
    face = jnp.concatenate([face[:, : columns - 128], face[:, columns - 128 :] * inner], 1)
    gain = gain_ref[members * low : members * (low + count)]
    return h + gain * ((flux[members:] - flux[:size]) + (face - pltpu.roll(face, 1, 1)))


def soil_tables(kinds, ks_ref, alpha_ref):
    ks = jnp.zeros(kinds.shape, jnp.float32)
    alpha = jnp.zeros(kinds.shape, jnp.float32)
    for t in range(SOIL_TYPES):
        ks = jnp.where(kinds == t, 0.5 * ks_ref[t], ks)
        alpha = jnp.where(kinds == t, alpha_ref[t] / LN2, alpha)
    return ks, alpha


def rule(h, ks_ref, alpha_ref, low, count, members):
    def wide(rows):
        return jnp.concatenate([jnp.broadcast_to(x, (members, x.shape[1])) for x in rows], 0)

    alpha = [alpha_ref[r : r + 1] for r in range(low, low + count)]
    return law(
        h,
        wide([ks_ref[r : r + 1] for r in range(low, low + count)]),
        wide(alpha),
        wide([(4.0 * LN2) * x for x in alpha]),
    )


def inner_mask():
    return (lax.broadcasted_iota(jnp.int32, (1, 128), 1) < 127).astype(jnp.float32)


def interior_kernel(heads_ref, tables_ref, out_ref, saved_ref, given, h0, h1, k0, k1, g0, g1, sems, in_sems, save_sems):
    members, rows, columns = given.shape
    ks_ref, alpha_ref = tables_ref.at[0:rows], tables_ref.at[rows:]
    tile = 8
    loads = [
        pltpu.make_async_copy(heads_ref.at[:, t : t + tile], given.at[:, t : t + tile], in_sems.at[t // tile])
        for t in range(0, rows, tile)
    ]
    for load in loads:
        load.start()
    inner = inner_mask()
    at = lambda r, n: slice(members * r, members * (r + n))
    for r in range(0, rows, 2):
        if r % tile == 0:
            loads[r // tile].wait()
        h = jnp.concatenate([given[:, r, :], given[:, r + 1, :]], 0)
        h0[at(r, 2)] = h
        k0[at(r, 2)], g0[at(r, 2)] = rule(h, ks_ref, alpha_ref, r, 2, members)
    now, later = (h0, k0, g0), (h1, k1, g1)
    copies = []

    def keep(ref, low, count, to):
        copies.append(pltpu.make_async_copy(ref.at[at(low, count)], saved_ref.at[at(to, count)], save_sems.at[len(copies)]))
        copies[-1].start()

    for step in range(1, MODEL_STEPS + 1):
        for low in range(step, rows - step, UNROLL):
            count = min(UNROLL, rows - step - low)
            h = moved(*now, low, count, members, inner)
            later[0][at(low, count)] = h
            if step < MODEL_STEPS:
                later[1][at(low, count)], later[2][at(low, count)] = rule(h, ks_ref, alpha_ref, low, count, members)
            else:
                for r in range(low, low + count):
                    copies.append(pltpu.make_async_copy(later[0].at[at(r, 1)], out_ref.at[r], sems.at[r]))
                    copies[-1].start()
        if step == 2:
            keep(h0, 0, 4, 0)
            keep(h0, rows - 4, 4, 4)
            keep(h1, 1, 2, 8)
            keep(h1, rows - 3, 2, 10)
        now, later = later, now
    for copy in copies:
        copy.wait()


def edge_kernel(above_ref, below_ref, saved_ref, tables_ref, given_ref, out_ref, *scratch):
    del given_ref
    *states, ks_ref, alpha_ref, sems = scratch
    rows = tables_ref.shape[0] // 2
    members = saved_ref.shape[0] // 12
    inner = inner_mask()
    cut = HALO * members
    at = lambda r, n: slice(members * r, members * (r + n))
    side = HALO + 4
    for n, ref in ((0, ks_ref), (1, alpha_ref)):
        far = slice(cut + HALO * n, cut + HALO * n + HALO)
        ref[0:HALO] = above_ref[far]
        ref[HALO:side] = tables_ref[rows * n : rows * n + 4]
        ref[side : side + 4] = tables_ref[rows * n + rows - 4 : rows * n + rows]
        ref[side + 4 : 2 * side] = below_ref[far]
    flag = slice(cut + 2 * HALO, cut + 2 * HALO + 1)
    has_above, has_below = above_ref[flag], below_ref[flag]

    def put(h, step, low, count):
        table = low + step if low < 5 else side + low - 5 + 2 - step
        k, g = rule(h, ks_ref, alpha_ref, table, count, members)
        states[3 * step + 1][at(low, count)] = k
        for j in range(count):
            row = g[members * j : members * (j + 1)]
            if table + j < HALO:
                row = row * has_above
            if table + j >= side + 4:
                row = row * has_below
            states[3 * step + 2][at(low + j, 1)] = row

    h = [states[3 * step] for step in range(MODEL_STEPS)]
    h[0][at(0, HALO)] = above_ref[0:cut]
    h[0][at(7, HALO)] = below_ref[0:cut]
    put(h[0][at(0, HALO)], 0, 0, HALO)
    put(h[0][at(7, HALO)], 0, 7, HALO)
    for step in range(MODEL_STEPS):
        for low, source in zip((3, 5), ((0, 6), (8, 10), (2, 4))[step]):
            kept = saved_ref[at(source, 2)]
            h[step][at(low, 2)] = kept
            put(kept, step, low, 2)
    copies = []
    for step in range(MODEL_STEPS):
        for low in (1, 6):
            new = moved(*states[3 * step : 3 * step + 3], low, HALO, members, inner)
            if step < MODEL_STEPS - 1:
                to = 0 if low == 1 else 7
                h[step + 1][at(to, HALO)] = new
                put(new, step + 1, to, HALO)
                continue
            row = 0 if low == 1 else rows - HALO
            h[0][at(low, HALO)] = new
            for j in range(HALO):
                copies.append(pltpu.make_async_copy(h[0].at[at(low + j, 1)], out_ref.at[row + j], sems.at[len(copies)]))
                copies[-1].start()
    for copy in copies:
        copy.wait()


def forecast(heads, soil_index, ks_table, alpha_table):
    members, rows, columns = heads.shape
    count = lax.axis_size("dev")
    far = pl.BlockSpec(memory_space=pltpu.HBM)
    near = pl.BlockSpec(memory_space=pltpu.VMEM)
    edge = jax.ShapeDtypeStruct((HALO * members + 8, columns), jnp.float32)
    table = jax.ShapeDtypeStruct((2 * rows, columns), jnp.float32)
    block = pltpu.VMEM((members, 8, columns), jnp.float32)
    limit = lambda mib: pltpu.CompilerParams(vmem_limit_bytes=mib * 2**20)
    top, bottom, tables = pl.pallas_call(
        edges_kernel,
        out_shape=(edge, edge, table),
        in_specs=[far] * 4,
        out_specs=(near, near, near),
        scratch_shapes=[pltpu.SMEM((SOIL_TYPES,), jnp.float32)] * 2
        + [pltpu.VMEM((rows, columns), jnp.int32), block, block, pltpu.SemaphoreType.DMA((5,))],
        compiler_params=limit(60),
        name="edges",
    )(ks_table, alpha_table, heads, soil_index)
    above = lax.ppermute(bottom, "dev", [(i, i + 1) for i in range(count - 1)])
    below = lax.ppermute(top, "dev", [(i + 1, i) for i in range(count - 1)])
    state = lambda r: pltpu.VMEM((r * members, columns), jnp.float32)
    by_row = jax.ShapeDtypeStruct((rows, members, columns), jnp.float32)
    inside, saved = pl.pallas_call(
        interior_kernel,
        out_shape=(by_row, jax.ShapeDtypeStruct((12 * members, columns), jnp.float32)),
        in_specs=[far, near],
        out_specs=(far, near),
        scratch_shapes=[pltpu.VMEM((members, rows, columns), jnp.float32)]
        + [state(rows)] * 6
        + [pltpu.SemaphoreType.DMA((rows,)), pltpu.SemaphoreType.DMA((rows // 8,)), pltpu.SemaphoreType.DMA((4,))],
        compiler_params=limit(FORECAST_MIB),
        cost_estimate=pl.CostEstimate(flops=60_000_000, bytes_accessed=5_000_000, transcendentals=4_000_000),
        name="interior",
    )(heads, tables)
    return pl.pallas_call(
        edge_kernel,
        out_shape=by_row,
        in_specs=[near] * 4 + [far],
        out_specs=far,
        scratch_shapes=[state(10)] * (3 * MODEL_STEPS)
        + [pltpu.VMEM((2 * (HALO + 4), columns), jnp.float32)] * 2
        + [pltpu.SemaphoreType.DMA((2 * HALO,))],
        input_output_aliases={4: 0},
        compiler_params=limit(FORECAST_MIB),
        name="edge",
    )(above, below, saved, tables, inside)


def along_z(k):
    groups, count = lax.axis_size("group"), lax.axis_size("dev")
    top = count // 2
    pairs = []
    for g in range(groups):
        for d in range(count):
            z = (2 * (d // top) + g % 2 + k) % 4
            pairs.append((g * count + d, (g // 2 * 2 + z % 2) * count + z // 2 * top + d % top))
    return pairs


def total_over_devices(x):
    count = lax.axis_size("dev")
    groups = lax.axis_size("group")
    rows = x.shape[0] // 2
    core = lax.axis_index("dev") % 2
    other = [(i, i ^ 1) for i in range(count)]
    low, high = x[:rows], x[rows:]
    mine = jnp.where(core == 0, low, high)
    x = mine + lax.ppermute(jnp.where(core == 0, high, low), "dev", other)

    def turned(size, base, k, n):
        if base == 0:
            return along_z(k)
        return [(i, i + (((i // base + k) % size) - (i // base) % size) * base) for i in range(n)]

    for axis, n, base, size in (
        ("dev", count, 2, 4),
        ("group", groups, 2, groups // 2),
        (AXES, groups * count, 0, 4),
    ):
        arrived = [lax.ppermute(x, axis, turned(size, base, k, n)) for k in range(1, size)]
        for a in arrived:
            x = x + a
    o = lax.ppermute(x, "dev", other)
    return jnp.concatenate([jnp.where(core == 0, x, o), jnp.where(core == 0, o, x)], axis=0)


def halves(x):
    high = x.astype(jnp.bfloat16)
    return high, (x - high.astype(jnp.float32)).astype(jnp.bfloat16)


def product(a, b, dims):
    (ah, al), (bh, bl) = a, b
    dot = lambda u, v: lax.dot_general(u, v, (dims, ((), ())), preferred_element_type=jnp.float32)
    return dot(ah, bh) + (dot(ah, bl) + dot(al, bh))


NN, NT, TN = ((1,), (0,)), ((1,), (1,)), ((0,), (0,))


def gram_kernel(mask_ref, op_ref, values_ref, heads_ref, spread_ref, packed_ref, joint_ref):
    sources, share, members, columns = spread_ref.shape
    total = sources * members
    lane = lax.broadcasted_iota(jnp.int32, (OBS, 256), 1)
    for r in range(share):
        whole = [heads_ref[s, r] for s in range(sources)]
        acc = whole[0]
        for s in range(1, sources):
            acc = acc + whole[s]
        mean = jnp.sum(acc, axis=0, keepdims=True) / total
        parts = []
        for s in range(sources):
            part = whole[s] - mean
            spread_ref[s, r] = part
            parts.append(part)
        parts.append(jnp.broadcast_to(mean, (8, columns)))
        rows = jnp.concatenate(parts, axis=0)
        for b in range(BLOCKS):
            at = r * BLOCKS + b
            high, low = halves(rows[:, 128 * b : 128 * b + 128])
            on = (mask_ref[r, b] != 0).astype(jnp.float32)
            op_high, op_low = halves(op_ref[at] * on)
            left = jnp.concatenate(
                [
                    jnp.concatenate([op_high, op_high], 1),
                    jnp.concatenate([op_low, jnp.zeros_like(op_low)], 1),
                ],
                0,
            )
            right = jnp.concatenate([high, low], 1)
            out = lax.dot_general(left, right, (NT, ((), ())), preferred_element_type=jnp.float32)
            out = out[:OBS] + out[OBS:]
            out = jnp.pad(out, ((0, 0), (0, 256 - out.shape[1])))
            innovation = values_ref[:, at : at + 1] * on - out
            joint = jnp.where(lane < total, out, jnp.where(lane == total, innovation, 0.0))
            joint_ref[OBS * at : OBS * at + OBS, :] = joint
    both = halves(joint_ref[...])
    gram = product(both, both, TN)
    side = lax.broadcasted_iota(jnp.int32, (64, 128), 1)
    down = lax.broadcasted_iota(jnp.int32, (64, 128), 0)
    turned = pltpu.roll(gram[64:128, :128], 64, 1)
    corner = pltpu.roll(gram[128:192, 128:], 64, 1)
    packed_ref[0:64] = jnp.where(side < 64, jnp.where(down >= side, gram[0:64, :128], turned), corner)
    packed_ref[64:128] = gram[128:192, :128]
    packed_ref[128:160] = jnp.where(side[:32] < 64, gram[64:96, :128], turned[32:])
    packed_ref[160:168] = gram[192:200, :128]
    diagonal = jnp.sum(jnp.where(down + 64 == side, gram[64:128, :128], 0.0), axis=0, keepdims=True)
    packed_ref[168:176] = jnp.where(side[:8] < 64, gram[192:200, 128:], jnp.broadcast_to(diagonal, (8, 128)))


def mean_and_gram(heads, op, mask, values):
    sources, share, members, columns = heads.shape
    anywhere = pl.BlockSpec(memory_space=pltpu.VMEM)
    return pl.pallas_call(
        gram_kernel,
        out_shape=(
            jax.ShapeDtypeStruct(heads.shape, jnp.float32),
            jax.ShapeDtypeStruct((176, 128), jnp.float32),
        ),
        in_specs=[pl.BlockSpec(memory_space=pltpu.SMEM), anywhere, anywhere] + [anywhere],
        out_specs=(anywhere, anywhere),
        scratch_shapes=[pltpu.VMEM((share * BLOCKS * OBS, 256), jnp.float32)],
        compiler_params=pltpu.CompilerParams(vmem_limit_bytes=40 * 2**20),
        name="gram",
    )(mask, op, values, heads)


def newton_kernel(packed_ref, out_ref, gram_ref):
    order = MEMBERS
    side = lax.broadcasted_iota(jnp.int32, (64, 128), 1)
    down = lax.broadcasted_iota(jnp.int32, (64, 128), 0)
    p0, p1, p2 = packed_ref[0:64], packed_ref[64:128], packed_ref[128:160]
    lower = jnp.concatenate([p2, pltpu.roll(p2, 64, 1)], 0)
    turned = jnp.concatenate([p0, lower], 0).T[0:64]
    diagonal = jnp.broadcast_to(pltpu.roll(packed_ref[168:176], 64, 1)[0:1], (64, 128))
    second = jnp.where(down < side, p0, jnp.where(down == side, diagonal, turned))
    gram_ref[0:64, 0:128] = jnp.where((side < 64) & (down >= side), p0, turned)
    gram_ref[64:128, 0:128] = jnp.where(side < 64, lower, pltpu.roll(second, 64, 1))
    gram_ref[128:192, 0:128] = p1
    gram_ref[0:128, 128:192] = p1.T
    gram_ref[128:192, 128:192] = pltpu.roll(p0, 64, 1)[:, :64]
    eye = (
        lax.broadcasted_iota(jnp.int32, (order, order), 0)
        == lax.broadcasted_iota(jnp.int32, (order, order), 1)
    ).astype(jnp.float32)
    gram = gram_ref[...] + (MEMBERS - 1.0) * eye
    rhs = jnp.concatenate([packed_ref[160:168], packed_ref[168:176, :64]], 1)
    norm = jnp.sum(jnp.abs(gram), keepdims=True)
    inverse_norm = 1.0 / norm
    iterate = gram * inverse_norm
    middle = 1.5 * eye - 0.5 * iterate
    iterate = product(halves(iterate), halves(middle), NN)
    inverse = middle
    for step in range(1, NEWTON_STEPS):
        left = halves(inverse)
        middle = 1.5 * eye - 0.5 * product(left, halves(iterate), NN)
        right = halves(middle)
        if step < NEWTON_STEPS - 1:
            iterate = product(halves(iterate), right, NN)
        inverse = product(left, right, NN)
    final = halves(inverse)
    shift = product(halves(product(halves(rhs), final, NN)), final, NN) * inverse_norm
    out_ref[...] = jnp.sqrt((MEMBERS - 1.0) * inverse_norm) * inverse + shift[0:1]


def newton_weights(packed):
    return pl.pallas_call(
        newton_kernel,
        out_shape=jax.ShapeDtypeStruct((MEMBERS, MEMBERS), jnp.float32),
        in_specs=[pl.BlockSpec(memory_space=pltpu.VMEM)],
        out_specs=pl.BlockSpec(memory_space=pltpu.VMEM),
        scratch_shapes=[pltpu.VMEM((MEMBERS, MEMBERS), jnp.float32)],
        compiler_params=pltpu.CompilerParams(vmem_limit_bytes=40 * 2**20),
        name="newton",
    )(packed)


def mix_kernel(weights_ref, spread_ref, out_ref):
    sources, share, members, columns = spread_ref.shape
    weights = halves(weights_ref[...])
    for r in range(share):
        for c in range(0, columns, 256):
            s = jnp.concatenate([spread_ref[g, r, :, c : c + 256] for g in range(sources)], 0)
            mixed = product(weights, halves(s), NN)
            for g in range(sources):
                out_ref[g, r, :, c : c + 256] = mixed[members * g : members * g + members]


def mix(weights, spread):
    anywhere = pl.BlockSpec(memory_space=pltpu.VMEM)
    return pl.pallas_call(
        mix_kernel,
        out_shape=jax.ShapeDtypeStruct(spread.shape, jnp.float32),
        in_specs=[anywhere, anywhere],
        out_specs=anywhere,
        compiler_params=pltpu.CompilerParams(vmem_limit_bytes=40 * 2**20),
        name="mix",
    )(weights, spread)


def body(member_pressure_heads, soil_index, ks_table, alpha_table, obs_op, obs_mask, obs_values):
    members, rows, columns = member_pressure_heads.shape
    groups = lax.axis_size("group")
    share = rows // groups
    predicted = forecast(member_pressure_heads, soil_index, ks_table, alpha_table)
    heads = lax.all_to_all(predicted.reshape(groups, share, members, columns), "group", 0, 0, tiled=True)
    op = obs_op.reshape(share * BLOCKS, OBS, 128)
    values = obs_values.reshape(share * BLOCKS, OBS).T
    spread, part = mean_and_gram(heads, op, obs_mask, values)
    mixed = mix(newton_weights(total_over_devices(part)), spread)
    back = lax.all_to_all(mixed, "group", 0, 0, tiled=True)
    return jnp.transpose(back.reshape(rows, members, columns), (1, 0, 2))


def solution(mesh):
    placed = (
        P("group", "dev", None),
        P("dev", None),
        P(),
        P(),
        P(("dev", "group"), None, None, None),
        P(("dev", "group"), None),
        P(("dev", "group"), None, None),
    )
    return jax.shard_map(
        body, mesh=mesh, in_specs=placed, out_specs=P("group", "dev", None), check_vma=False
    )
```

```python
import jax
import jax.numpy as jnp
from jax import lax
from jax.experimental import pallas as pl
from jax.experimental.pallas import tpu as pltpu
from jax.sharding import PartitionSpec as P

MEMBERS = 192
SOIL_TYPES = 8
MODEL_STEPS = 3
NEWTON_STEPS = 12
BLOCKS = 6
OBS = 32

HALO = MODEL_STEPS
LN2 = 0.6931471805599453
UNROLL = 4
FORECAST_MIB = 32
gravity_head = 1.0
AXES = ("group", "dev")


def edges_kernel(ks_far, alpha_far, heads_ref, soil_far, top_ref, bottom_ref, tables_ref, ks_table, alpha_table, soil_ref, first, last, sems):
    members, span, columns = first.shape
    rows = soil_ref.shape[0]
    loads = [
        pltpu.make_async_copy(source, ref, sems.at[n])
        for n, (source, ref) in enumerate(
            (
                (ks_far, ks_table),
                (alpha_far, alpha_table),
                (soil_far, soil_ref),
                (heads_ref.at[:, 0:span], first),
                (heads_ref.at[:, rows - span : rows], last),
            )
        )
    ]
    for load in loads:
        load.start()
    for load in loads[:3]:
        load.wait()
    ks, alpha = soil_tables(soil_ref[...], ks_table, alpha_table)
    tables_ref[0:rows] = ks
    tables_ref[rows:] = alpha
    flag = jnp.ones((8 - 2 * HALO, columns), jnp.float32)
    top_ref[HALO * members :] = jnp.concatenate([ks[:HALO], alpha[:HALO], flag], 0)
    bottom_ref[HALO * members :] = jnp.concatenate([ks[rows - HALO :], alpha[rows - HALO :], flag], 0)
    for load in loads[3:]:
        load.wait()
    for j in range(HALO):
        top_ref[members * j : members * j + members] = first[:, j, :]
        bottom_ref[members * j : members * j + members] = last[:, span - HALO + j, :]


def law(h, ks, alpha, slope):
    factor = jnp.exp2(alpha * jnp.minimum(h, 0.0))
    return ks * factor, 1.0 / (1.0 + slope * factor)


def moved(h_ref, k_ref, gain_ref, low, count, members, inner):
    size = members * count
    around = slice(members * (low - 1), members * (low + count + 1))
    h_all, k_all = h_ref[around], k_ref[around]
    columns = h_all.shape[1]
    flux = (k_all[members:] + k_all[:-members]) * (h_all[members:] - h_all[:-members])
    h, k = h_all[members : members + size], k_all[members : members + size]
    face = (k + pltpu.roll(k, columns - 1, 1)) * ((pltpu.roll(h, columns - 1, 1) - gravity_head) - h)
    face = jnp.concatenate([face[:, : columns - 128], face[:, columns - 128 :] * inner], 1)
    gain = gain_ref[members * low : members * (low + count)]
    return h + gain * ((flux[members:] - flux[:size]) + (face - pltpu.roll(face, 1, 1)))


def soil_tables(kinds, ks_ref, alpha_ref):
    ks = jnp.zeros(kinds.shape, jnp.float32)
    alpha = jnp.zeros(kinds.shape, jnp.float32)
    for t in range(SOIL_TYPES):
        ks = jnp.where(kinds == t, 0.5 * ks_ref[t], ks)
        alpha = jnp.where(kinds == t, alpha_ref[t] / LN2, alpha)
    return ks, alpha


def rule(h, ks_ref, alpha_ref, low, count, members):
    def wide(rows):
        return jnp.concatenate([jnp.broadcast_to(x, (members, x.shape[1])) for x in rows], 0)

    alpha = [alpha_ref[r : r + 1] for r in range(low, low + count)]
    return law(
        h,
        wide([ks_ref[r : r + 1] for r in range(low, low + count)]),
        wide(alpha),
        wide([(4.0 * LN2) * x for x in alpha]),
    )


def inner_mask():
    return (lax.broadcasted_iota(jnp.int32, (1, 128), 1) < 127).astype(jnp.float32)


def interior_kernel(heads_ref, tables_ref, out_ref, saved_ref, given, h0, h1, k0, k1, g0, g1, sems, in_sems, save_sems):
    members, rows, columns = given.shape
    ks_ref, alpha_ref = tables_ref.at[0:rows], tables_ref.at[rows:]
    tile = 8
    loads = [
        pltpu.make_async_copy(heads_ref.at[:, t : t + tile], given.at[:, t : t + tile], in_sems.at[t // tile])
        for t in range(0, rows, tile)
    ]
    for load in loads:
        load.start()
    inner = inner_mask()
    at = lambda r, n: slice(members * r, members * (r + n))
    for r in range(0, rows, 2):
        if r % tile == 0:
            loads[r // tile].wait()
        h = jnp.concatenate([given[:, r, :], given[:, r + 1, :]], 0)
        h0[at(r, 2)] = h
        k0[at(r, 2)], g0[at(r, 2)] = rule(h, ks_ref, alpha_ref, r, 2, members)
    now, later = (h0, k0, g0), (h1, k1, g1)
    copies = []

    def keep(ref, low, count, to):
        copies.append(pltpu.make_async_copy(ref.at[at(low, count)], saved_ref.at[at(to, count)], save_sems.at[len(copies)]))
        copies[-1].start()

    for step in range(1, MODEL_STEPS + 1):
        for low in range(step, rows - step, UNROLL):
            count = min(UNROLL, rows - step - low)
            h = moved(*now, low, count, members, inner)
            later[0][at(low, count)] = h
            if step < MODEL_STEPS:
                later[1][at(low, count)], later[2][at(low, count)] = rule(h, ks_ref, alpha_ref, low, count, members)
            else:
                for r in range(low, low + count):
                    copies.append(pltpu.make_async_copy(later[0].at[at(r, 1)], out_ref.at[r], sems.at[r]))
                    copies[-1].start()
        if step == 2:
            keep(h0, 0, 4, 0)
            keep(h0, rows - 4, 4, 4)
            keep(h1, 1, 2, 8)
            keep(h1, rows - 3, 2, 10)
        now, later = later, now
    for copy in copies:
        copy.wait()


def edge_kernel(above_ref, below_ref, saved_ref, tables_ref, given_ref, out_ref, *scratch):
    del given_ref
    *states, ks_ref, alpha_ref, sems = scratch
    rows = tables_ref.shape[0] // 2
    members = saved_ref.shape[0] // 12
    inner = inner_mask()
    cut = HALO * members
    at = lambda r, n: slice(members * r, members * (r + n))
    side = HALO + 4
    for n, ref in ((0, ks_ref), (1, alpha_ref)):
        far = slice(cut + HALO * n, cut + HALO * n + HALO)
        ref[0:HALO] = above_ref[far]
        ref[HALO:side] = tables_ref[rows * n : rows * n + 4]
        ref[side : side + 4] = tables_ref[rows * n + rows - 4 : rows * n + rows]
        ref[side + 4 : 2 * side] = below_ref[far]
    flag = slice(cut + 2 * HALO, cut + 2 * HALO + 1)
    has_above, has_below = above_ref[flag], below_ref[flag]

    def put(h, step, low, count):
        table = low + step if low < 5 else side + low - 5 + 2 - step
        k, g = rule(h, ks_ref, alpha_ref, table, count, members)
        states[3 * step + 1][at(low, count)] = k
        for j in range(count):
            row = g[members * j : members * (j + 1)]
            if table + j < HALO:
                row = row * has_above
            if table + j >= side + 4:
                row = row * has_below
            states[3 * step + 2][at(low + j, 1)] = row

    h = [states[3 * step] for step in range(MODEL_STEPS)]
    h[0][at(0, HALO)] = above_ref[0:cut]
    h[0][at(7, HALO)] = below_ref[0:cut]
    put(h[0][at(0, HALO)], 0, 0, HALO)
    put(h[0][at(7, HALO)], 0, 7, HALO)
    for step in range(MODEL_STEPS):
        for low, source in zip((3, 5), ((0, 6), (8, 10), (2, 4))[step]):
            kept = saved_ref[at(source, 2)]
            h[step][at(low, 2)] = kept
            put(kept, step, low, 2)
    copies = []
    for step in range(MODEL_STEPS):
        for low in (1, 6):
            new = moved(*states[3 * step : 3 * step + 3], low, HALO, members, inner)
            if step < MODEL_STEPS - 1:
                to = 0 if low == 1 else 7
                h[step + 1][at(to, HALO)] = new
                put(new, step + 1, to, HALO)
                continue
            row = 0 if low == 1 else rows - HALO
            h[0][at(low, HALO)] = new
            for j in range(HALO):
                copies.append(pltpu.make_async_copy(h[0].at[at(low + j, 1)], out_ref.at[row + j], sems.at[len(copies)]))
                copies[-1].start()
    for copy in copies:
        copy.wait()


def forecast(heads, soil_index, ks_table, alpha_table):
    members, rows, columns = heads.shape
    count = lax.axis_size("dev")
    far = pl.BlockSpec(memory_space=pltpu.HBM)
    near = pl.BlockSpec(memory_space=pltpu.VMEM)
    edge = jax.ShapeDtypeStruct((HALO * members + 8, columns), jnp.float32)
    table = jax.ShapeDtypeStruct((2 * rows, columns), jnp.float32)
    block = pltpu.VMEM((members, 8, columns), jnp.float32)
    limit = lambda mib: pltpu.CompilerParams(vmem_limit_bytes=mib * 2**20)
    top, bottom, tables = pl.pallas_call(
        edges_kernel,
        out_shape=(edge, edge, table),
        in_specs=[far] * 4,
        out_specs=(near, near, near),
        scratch_shapes=[pltpu.SMEM((SOIL_TYPES,), jnp.float32)] * 2
        + [pltpu.VMEM((rows, columns), jnp.int32), block, block, pltpu.SemaphoreType.DMA((5,))],
        compiler_params=limit(60),
        name="edges",
    )(ks_table, alpha_table, heads, soil_index)
    above = lax.ppermute(bottom, "dev", [(i, i + 1) for i in range(count - 1)])
    below = lax.ppermute(top, "dev", [(i + 1, i) for i in range(count - 1)])
    state = lambda r: pltpu.VMEM((r * members, columns), jnp.float32)
    by_row = jax.ShapeDtypeStruct((rows, members, columns), jnp.float32)
    inside, saved = pl.pallas_call(
        interior_kernel,
        out_shape=(by_row, jax.ShapeDtypeStruct((12 * members, columns), jnp.float32)),
        in_specs=[far, near],
        out_specs=(far, near),
        scratch_shapes=[pltpu.VMEM((members, rows, columns), jnp.float32)]
        + [state(rows)] * 6
        + [pltpu.SemaphoreType.DMA((rows,)), pltpu.SemaphoreType.DMA((rows // 8,)), pltpu.SemaphoreType.DMA((4,))],
        compiler_params=limit(FORECAST_MIB),
        cost_estimate=pl.CostEstimate(flops=60_000_000, bytes_accessed=5_000_000, transcendentals=4_000_000),
        name="interior",
    )(heads, tables)
    return pl.pallas_call(
        edge_kernel,
        out_shape=by_row,
        in_specs=[near] * 4 + [far],
        out_specs=far,
        scratch_shapes=[state(10)] * (3 * MODEL_STEPS)
        + [pltpu.VMEM((2 * (HALO + 4), columns), jnp.float32)] * 2
        + [pltpu.SemaphoreType.DMA((2 * HALO,))],
        input_output_aliases={4: 0},
        compiler_params=limit(FORECAST_MIB),
        name="edge",
    )(above, below, saved, tables, inside)


def along_z(k):
    groups, count = lax.axis_size("group"), lax.axis_size("dev")
    top = count // 2
    pairs = []
    for g in range(groups):
        for d in range(count):
            z = (2 * (d // top) + g % 2 + k) % 4
            pairs.append((g * count + d, (g // 2 * 2 + z % 2) * count + z // 2 * top + d % top))
    return pairs


def total_over_devices(x):
    count = lax.axis_size("dev")
    groups = lax.axis_size("group")
    rows = x.shape[0] // 2
    core = lax.axis_index("dev") % 2
    other = [(i, i ^ 1) for i in range(count)]
    low, high = x[:rows], x[rows:]
    mine = jnp.where(core == 0, low, high)
    x = mine + lax.ppermute(jnp.where(core == 0, high, low), "dev", other)

    def turned(size, base, k, n):
        if base == 0:
            return along_z(k)
        return [(i, i + (((i // base + k) % size) - (i // base) % size) * base) for i in range(n)]

    for axis, n, base, size in (
        (AXES, groups * count, 0, 4),
        ("group", groups, 2, groups // 2),
        ("dev", count, 2, 4),
    ):
        arrived = [lax.ppermute(x, axis, turned(size, base, k, n)) for k in range(1, size)]
        for a in arrived:
            x = x + a
    o = lax.ppermute(x, "dev", other)
    return jnp.concatenate([jnp.where(core == 0, x, o), jnp.where(core == 0, o, x)], axis=0)


def halves(x):
    high = x.astype(jnp.bfloat16)
    return high, (x - high.astype(jnp.float32)).astype(jnp.bfloat16)


def product(a, b, dims):
    (ah, al), (bh, bl) = a, b
    dot = lambda u, v: lax.dot_general(u, v, (dims, ((), ())), preferred_element_type=jnp.float32)
    return dot(ah, bh) + (dot(ah, bl) + dot(al, bh))


NN, NT, TN = ((1,), (0,)), ((1,), (1,)), ((0,), (0,))


def gram_kernel(mask_ref, op_ref, values_ref, heads_ref, spread_ref, packed_ref, joint_ref):
    sources, share, members, columns = spread_ref.shape
    total = sources * members
    lane = lax.broadcasted_iota(jnp.int32, (OBS, 256), 1)
    for r in range(share):
        whole = [heads_ref[s, r] for s in range(sources)]
        acc = whole[0]
        for s in range(1, sources):
            acc = acc + whole[s]
        mean = jnp.sum(acc, axis=0, keepdims=True) / total
        parts = []
        for s in range(sources):
            part = whole[s] - mean
            spread_ref[s, r] = part
            parts.append(part)
        parts.append(jnp.broadcast_to(mean, (8, columns)))
        rows = jnp.concatenate(parts, axis=0)
        for b in range(BLOCKS):
            at = r * BLOCKS + b
            high, low = halves(rows[:, 128 * b : 128 * b + 128])
            on = (mask_ref[r, b] != 0).astype(jnp.float32)
            op_high, op_low = halves(op_ref[at] * on)
            left = jnp.concatenate(
                [
                    jnp.concatenate([op_high, op_high], 1),
                    jnp.concatenate([op_low, jnp.zeros_like(op_low)], 1),
                ],
                0,
            )
            right = jnp.concatenate([high, low], 1)
            out = lax.dot_general(left, right, (NT, ((), ())), preferred_element_type=jnp.float32)
            out = out[:OBS] + out[OBS:]
            out = jnp.pad(out, ((0, 0), (0, 256 - out.shape[1])))
            innovation = values_ref[:, at : at + 1] * on - out
            joint = jnp.where(lane < total, out, jnp.where(lane == total, innovation, 0.0))
            joint_ref[OBS * at : OBS * at + OBS, :] = joint
    both = halves(joint_ref[...])
    gram = product(both, both, TN)
    side = lax.broadcasted_iota(jnp.int32, (64, 128), 1)
    down = lax.broadcasted_iota(jnp.int32, (64, 128), 0)
    turned = pltpu.roll(gram[64:128, :128], 64, 1)
    corner = pltpu.roll(gram[128:192, 128:], 64, 1)
    packed_ref[0:64] = jnp.where(side < 64, jnp.where(down >= side, gram[0:64, :128], turned), corner)
    packed_ref[64:128] = gram[128:192, :128]
    packed_ref[128:160] = jnp.where(side[:32] < 64, gram[64:96, :128], turned[32:])
    packed_ref[160:168] = gram[192:200, :128]
    diagonal = jnp.sum(jnp.where(down + 64 == side, gram[64:128, :128], 0.0), axis=0, keepdims=True)
    packed_ref[168:176] = jnp.where(side[:8] < 64, gram[192:200, 128:], jnp.broadcast_to(diagonal, (8, 128)))


def mean_and_gram(heads, op, mask, values):
    sources, share, members, columns = heads.shape
    anywhere = pl.BlockSpec(memory_space=pltpu.VMEM)
    return pl.pallas_call(
        gram_kernel,
        out_shape=(
            jax.ShapeDtypeStruct(heads.shape, jnp.float32),
            jax.ShapeDtypeStruct((176, 128), jnp.float32),
        ),
        in_specs=[pl.BlockSpec(memory_space=pltpu.SMEM), anywhere, anywhere] + [anywhere],
        out_specs=(anywhere, anywhere),
        scratch_shapes=[pltpu.VMEM((share * BLOCKS * OBS, 256), jnp.float32)],
        compiler_params=pltpu.CompilerParams(vmem_limit_bytes=40 * 2**20),
        name="gram",
    )(mask, op, values, heads)


def newton_kernel(packed_ref, out_ref, gram_ref):
    order = MEMBERS
    side = lax.broadcasted_iota(jnp.int32, (64, 128), 1)
    down = lax.broadcasted_iota(jnp.int32, (64, 128), 0)
    p0, p1, p2 = packed_ref[0:64], packed_ref[64:128], packed_ref[128:160]
    lower = jnp.concatenate([p2, pltpu.roll(p2, 64, 1)], 0)
    turned = jnp.concatenate([p0, lower], 0).T[0:64]
    diagonal = jnp.broadcast_to(pltpu.roll(packed_ref[168:176], 64, 1)[0:1], (64, 128))
    second = jnp.where(down < side, p0, jnp.where(down == side, diagonal, turned))
    gram_ref[0:64, 0:128] = jnp.where((side < 64) & (down >= side), p0, turned)
    gram_ref[64:128, 0:128] = jnp.where(side < 64, lower, pltpu.roll(second, 64, 1))
    gram_ref[128:192, 0:128] = p1
    gram_ref[0:128, 128:192] = p1.T
    gram_ref[128:192, 128:192] = pltpu.roll(p0, 64, 1)[:, :64]
    eye = (
        lax.broadcasted_iota(jnp.int32, (order, order), 0)
        == lax.broadcasted_iota(jnp.int32, (order, order), 1)
    ).astype(jnp.float32)
    gram = gram_ref[...] + (MEMBERS - 1.0) * eye
    rhs = jnp.concatenate([packed_ref[160:168], packed_ref[168:176, :64]], 1)
    norm = jnp.sum(jnp.abs(gram), keepdims=True)
    inverse_norm = 1.0 / norm
    iterate = gram * inverse_norm
    middle = 1.5 * eye - 0.5 * iterate
    iterate = product(halves(iterate), halves(middle), NN)
    inverse = middle
    for step in range(1, NEWTON_STEPS):
        left = halves(inverse)
        middle = 1.5 * eye - 0.5 * product(left, halves(iterate), NN)
        right = halves(middle)
        if step < NEWTON_STEPS - 1:
            iterate = product(halves(iterate), right, NN)
        inverse = product(left, right, NN)
    final = halves(inverse)
    shift = product(halves(product(halves(rhs), final, NN)), final, NN) * inverse_norm
    out_ref[...] = jnp.sqrt((MEMBERS - 1.0) * inverse_norm) * inverse + shift[0:1]


def newton_weights(packed):
    return pl.pallas_call(
        newton_kernel,
        out_shape=jax.ShapeDtypeStruct((MEMBERS, MEMBERS), jnp.float32),
        in_specs=[pl.BlockSpec(memory_space=pltpu.VMEM)],
        out_specs=pl.BlockSpec(memory_space=pltpu.VMEM),
        scratch_shapes=[pltpu.VMEM((MEMBERS, MEMBERS), jnp.float32)],
        compiler_params=pltpu.CompilerParams(vmem_limit_bytes=40 * 2**20),
        name="newton",
    )(packed)


def mix_kernel(weights_ref, spread_ref, out_ref):
    sources, share, members, columns = spread_ref.shape
    weights = halves(weights_ref[...])
    for r in range(share):
        for c in range(0, columns, 256):
            s = jnp.concatenate([spread_ref[g, r, :, c : c + 256] for g in range(sources)], 0)
            mixed = product(weights, halves(s), NN)
            for g in range(sources):
                out_ref[g, r, :, c : c + 256] = mixed[members * g : members * g + members]


def mix(weights, spread):
    anywhere = pl.BlockSpec(memory_space=pltpu.VMEM)
    return pl.pallas_call(
        mix_kernel,
        out_shape=jax.ShapeDtypeStruct(spread.shape, jnp.float32),
        in_specs=[anywhere, anywhere],
        out_specs=anywhere,
        compiler_params=pltpu.CompilerParams(vmem_limit_bytes=40 * 2**20),
        name="mix",
    )(weights, spread)


def body(member_pressure_heads, soil_index, ks_table, alpha_table, obs_op, obs_mask, obs_values):
    members, rows, columns = member_pressure_heads.shape
    groups = lax.axis_size("group")
    share = rows // groups
    predicted = forecast(member_pressure_heads, soil_index, ks_table, alpha_table)
    heads = lax.all_to_all(predicted.reshape(groups, share, members, columns), "group", 0, 0, tiled=True)
    op = obs_op.reshape(share * BLOCKS, OBS, 128)
    values = obs_values.reshape(share * BLOCKS, OBS).T
    spread, part = mean_and_gram(heads, op, obs_mask, values)
    mixed = mix(newton_weights(total_over_devices(part)), spread)
    back = lax.all_to_all(mixed, "group", 0, 0, tiled=True)
    return jnp.transpose(back.reshape(rows, members, columns), (1, 0, 2))


def solution(mesh):
    placed = (
        P("group", "dev", None),
        P("dev", None),
        P(),
        P(),
        P(("dev", "group"), None, None, None),
        P(("dev", "group"), None),
        P(("dev", "group"), None, None),
    )
    return jax.shard_map(
        body, mesh=mesh, in_specs=placed, out_specs=P("group", "dev", None), check_vma=False
    )
```
